256 devices in a mesh: dp: 64 (over x, z, core), tensor: 4 (over y).
Axes of the slice: x: 4, y: 4, z: 8, core: 2. Of those that a mesh axis runs over, the one named last changes fastest.
Arguments:
- queries: bfloat16 [24576, 8192], P('dp', 'tensor'), may hold values from -1100 to 1100
- keys: bfloat16 [24576, 1024], P('dp', 'tensor'), may hold values from -1100 to 1100
- values: bfloat16 [24576, 1024], P('dp', 'tensor'), may hold values from -6 to 6
- output_gradient: bfloat16 [24576, 8192], P('dp', 'tensor'), may hold values from -6 to 6
- q_gain: float32 [128], replicated, may hold values from 0.5 to 4.1
- k_gain: float32 [128], replicated, may hold values from 0.5 to 4.1
- prompt_len: int32 [64], P('dp'), may hold values from 1 to 256, as said below
- resp_len: int32 [128], P('dp'), may hold values from 1 to 64, as said below
- resp_owner: int32 [128], P('dp'), may hold values from 0 to 63, as said below
Outputs:
- q_grad: bfloat16 [24576, 8192], P('dp', 'tensor')
- k_grad: bfloat16 [24576, 1024], P('dp', 'tensor')
- v_grad: bfloat16 [24576, 1024], P('dp', 'tensor')
- q_gain_grad: float32 [128], replicated
- k_gain_grad: float32 [128], replicated
The draws below stay inside these ranges and needn't reach their ends.
Inputs may be any that keep to these rules, and one draw needn't show every extreme that they name: `prompt_len`: some prompt has length exactly 256. `resp_len`: some response has length exactly 64. Response s lies on dp index floor(s / 2); that index minus resp_owner[s], modulo the number of dp indices, is 1 to 4, and equals 4 for some response.
All inputs are finite; a program needn't handle non-finite values.
Results may differ from the reference program's by a relative error of at most 0.009.
The reference program's roundings to bfloat16 on the way count: a program that leaves them out, or rounds other values in their place, can miss the bound.
Values may be sent and summed in bfloat16 or wider, within the bound.
A program may use at most 128 MiB of HBM per device.

```python
import math
import jax
import jax.numpy as jnp
from jax import lax

QUERY_HEADS = 64
KEY_VALUE_HEADS = 8
HEAD_SIZE = 128
PROMPT_LENGTH = 256
RESPONSE_LENGTH = 64
RESPONSE_SLOTS = 2
REACH = 4
TOKEN_ROWS = 24576
SLOTS = 128
N_DP = 64


def entries_scaled(key, heads, score_entries, spread):
    first_key, second_key = jax.random.split(key)
    row_scale = jnp.exp(jax.random.uniform(first_key, (TOKEN_ROWS, 1), minval=0.0, maxval=math.log(spread)))
    col_scale = jnp.exp(jax.random.uniform(second_key, (1, heads * HEAD_SIZE), minval=0.0, maxval=math.log(spread)))
    return score_entries * row_scale * col_scale


def draw_queries(key, part):
    key = jax.random.fold_in(key, 11)
    entries_random_key, scale_random_key = jax.random.split(key, 2)
    score_entries = jax.random.truncated_normal(entries_random_key, -4.0, 4.0, (TOKEN_ROWS, QUERY_HEADS * HEAD_SIZE))
    sampled_draws = entries_scaled(scale_random_key, QUERY_HEADS, score_entries, 10.0)
    return sampled_draws.astype(jnp.bfloat16)


def draw_keys(key, part):
    key = jax.random.fold_in(key, 12)
    entries_random_key, scale_random_key = jax.random.split(key, 2)
    score_entries = jax.random.truncated_normal(entries_random_key, -4.0, 4.0, (TOKEN_ROWS, KEY_VALUE_HEADS * HEAD_SIZE))
    sampled_draws = entries_scaled(scale_random_key, KEY_VALUE_HEADS, score_entries, 10.0)
    return sampled_draws.astype(jnp.bfloat16)


def draw_q_gain(key, part):
    key = jax.random.fold_in(key, 13)
    sampled_draws = jnp.exp(jax.random.uniform(key, (HEAD_SIZE,), minval=math.log(0.5), maxval=math.log(2.0)))
    return sampled_draws


def draw_k_gain(key, part):
    key = jax.random.fold_in(key, 14)
    sampled_draws = jnp.exp(jax.random.uniform(key, (HEAD_SIZE,), minval=math.log(0.5), maxval=math.log(2.0)))
    return sampled_draws


def draw_prompt_len(key, part):
    key = jax.random.fold_in(key, 21)
    first_key, second_key = jax.random.split(key)
    lengths = jax.random.randint(first_key, (N_DP,), 1, PROMPT_LENGTH + 1)
    forced = jax.random.randint(second_key, (), 0, N_DP)
    return jnp.where(jnp.arange(N_DP) == forced, PROMPT_LENGTH, lengths).astype(jnp.int32)


def draw_resp_len(key, part):
    key = jax.random.fold_in(key, 22)
    first_key, second_key = jax.random.split(key)
    lengths = jax.random.randint(first_key, (SLOTS,), 1, RESPONSE_LENGTH + 1)
    forced = jax.random.randint(second_key, (), 0, SLOTS)
    return jnp.where(jnp.arange(SLOTS) == forced, RESPONSE_LENGTH, lengths).astype(jnp.int32)


def draw_resp_owner(key, part):
    key = jax.random.fold_in(key, 23)
    first_key, second_key = jax.random.split(key)
    distance = jax.random.randint(first_key, (SLOTS,), 1, REACH + 1)
    forced = jax.random.randint(second_key, (), RESPONSE_SLOTS + 1, SLOTS)
    slot_index = jnp.arange(SLOTS)
    distance = jnp.where(slot_index == forced, REACH, distance)
    distance = jnp.where((slot_index == 0) | (slot_index == RESPONSE_SLOTS), 1, distance)
    holder = slot_index // RESPONSE_SLOTS
    return ((holder - distance) % N_DP).astype(jnp.int32)


def block_levels(rng, shape, pieces, smallest, largest):
    gain = 1.0
    for axis_at, parts in pieces:
        heights = jax.random.uniform(jax.random.fold_in(jax.random.fold_in(rng, 6), axis_at), (parts,), jnp.float32, smallest / len(pieces), largest / len(pieces))
        gain = gain * jnp.repeat(jnp.exp(heights), shape[axis_at] // parts).reshape((-1,) + (1,) * (len(shape) - 1 - axis_at))
    return gain


def normal_values(own_key, extent, scale, reach, cuts=(), kind=jnp.bfloat16):
    gain = block_levels(own_key, extent, cuts, -0.22, 0.18) if cuts else 1.0
    entries = jax.random.normal(own_key, extent, jnp.float32) * scale * gain
    return jnp.minimum(jnp.maximum(entries, -reach), reach).astype(kind)


def setup_inputs(seed: int = 0) -> dict:
    splits = jax.random.split(jax.random.key(seed), 10)
    return {
        "queries": draw_queries(jax.random.fold_in(splits[9], 71), 0),
        "keys": draw_keys(jax.random.fold_in(splits[9], 71), 0),
        "values": normal_values(splits[2], (TOKEN_ROWS, KEY_VALUE_HEADS * HEAD_SIZE), 1.0, 6.0, ((0, 64), (1, 4))),
        "output_gradient": normal_values(splits[3], (TOKEN_ROWS, QUERY_HEADS * HEAD_SIZE), 1.0, 6.0, ((0, 64), (1, 4))),
        "q_gain": draw_q_gain(jax.random.fold_in(splits[9], 71), 0),
        "k_gain": draw_k_gain(jax.random.fold_in(splits[9], 71), 0),
        "prompt_len": draw_prompt_len(jax.random.fold_in(splits[9], 71), 0),
        "resp_len": draw_resp_len(jax.random.fold_in(splits[9], 71), 0),
        "resp_owner": draw_resp_owner(jax.random.fold_in(splits[9], 71), 0),
    }


EPSILON = 1e-06

def normalize(source, gain_vec):
    widened = source.astype(jnp.float32)
    inverse = lax.rsqrt(lax.optimization_barrier(jnp.mean(widened * widened, axis=-1, keepdims=True)) + EPSILON)
    return ((widened * inverse * gain_vec).astype(jnp.bfloat16), inverse)

def norm_backward(upstream, source, inverse, gain_vec):
    widened = source.astype(jnp.float32)
    scaled = upstream * gain_vec
    mean_term = lax.optimization_barrier(jnp.mean(scaled * widened, axis=-1, keepdims=True))
    result = inverse * scaled - widened * inverse ** 3 * mean_term
    gain_part = lax.optimization_barrier(jnp.sum((upstream * widened * inverse).reshape(-1, widened.shape[-1]), axis=0))
    return (result, gain_part)

def attend(q_rows, k_rows, v_rows, d_rows, allowed):
    exact = lax.Precision.HIGHEST
    score_scale = q_rows.shape[-1] ** (-0.5)
    q_wide = q_rows.astype(jnp.float32)
    k_wide = k_rows.astype(jnp.float32)
    v_wide = v_rows.astype(jnp.float32)
    d_wide = d_rows.astype(jnp.float32)
    scores = jnp.einsum('mgd,nd->gmn', q_wide, k_wide, precision=exact) * score_scale
    scores = jnp.where(allowed[None], scores, -jnp.inf)
    row_max = lax.optimization_barrier(jnp.max(scores, axis=-1, keepdims=True))
    raised = jnp.exp(scores - row_max)
    probability = raised / lax.optimization_barrier(jnp.sum(raised, axis=-1, keepdims=True))
    weights = lax.optimization_barrier(probability.astype(jnp.bfloat16)).astype(jnp.float32)
    output = jnp.einsum('gmn,nd->mgd', weights, v_wide, precision=exact)
    v_grad = jnp.einsum('gmn,mgd->nd', weights, d_wide, precision=exact)
    p_grad = jnp.einsum('mgd,nd->gmn', d_wide, v_wide, precision=exact)
    row_inner = jnp.einsum('mgd,mgd->gm', d_wide, output, precision=exact)[..., None]
    s_grad = (probability * (p_grad - row_inner) * score_scale).astype(jnp.bfloat16)
    s_grad = lax.optimization_barrier(s_grad).astype(jnp.float32)
    q_grad = jnp.einsum('gmn,nd->mgd', s_grad, k_wide, precision=exact)
    k_grad = jnp.einsum('gmn,mgd->nd', s_grad, q_wide, precision=exact)
    return (q_grad, k_grad, v_grad)

def reference(queries, keys, values, output_gradient, q_gain, k_gain, prompt_len, resp_len, resp_owner):
    row_total_count = PROMPT_LENGTH + RESPONSE_SLOTS * RESPONSE_LENGTH
    query_group_size = QUERY_HEADS // KEY_VALUE_HEADS
    slot_total_count = N_DP * RESPONSE_SLOTS
    query_unnormed = queries.reshape(N_DP, row_total_count, KEY_VALUE_HEADS, query_group_size, HEAD_SIZE)
    key_unnormed = keys.reshape(N_DP, row_total_count, KEY_VALUE_HEADS, HEAD_SIZE)
    value_row_block = values.reshape(N_DP, row_total_count, KEY_VALUE_HEADS, HEAD_SIZE)
    query_head_norm, query_inv = normalize(query_unnormed, q_gain)
    key_head_norm, key_inv = normalize(key_unnormed, k_gain)
    prompt_keep = jnp.arange(PROMPT_LENGTH)[None, :] < prompt_len[:, None]
    reply_keep = (jnp.arange(RESPONSE_LENGTH)[None, :] < resp_len[:, None]).reshape(N_DP, RESPONSE_SLOTS * RESPONSE_LENGTH)
    row_keep_mask = jnp.concatenate([prompt_keep, reply_keep], axis=1)
    gradient_rows = jnp.where(row_keep_mask[..., None, None, None], output_gradient.reshape(N_DP, row_total_count, KEY_VALUE_HEADS, query_group_size, HEAD_SIZE), jnp.zeros((), output_gradient.dtype))
    causal = jnp.arange(PROMPT_LENGTH)[None, :] <= jnp.arange(PROMPT_LENGTH)[:, None]
    own_part = jnp.arange(RESPONSE_LENGTH)[None, :] <= jnp.arange(RESPONSE_LENGTH)[:, None]
    per_head = jax.vmap(attend, in_axes=(1, 1, 1, 1, None), out_axes=(1, 1, 1))

    def prompt_device(inputs):
        q_rows, k_rows, v_rows, d_rows, length = inputs
        visible = causal & (jnp.arange(PROMPT_LENGTH)[None, :] < length)
        return per_head(q_rows, k_rows, v_rows, d_rows, visible)
    prompt_query_gradient, prompt_key_gradient, prompt_value_gradient = lax.map(prompt_device, (query_head_norm[:, :PROMPT_LENGTH], key_head_norm[:, :PROMPT_LENGTH], value_row_block[:, :PROMPT_LENGTH], gradient_rows[:, :PROMPT_LENGTH], prompt_len))
    response_queries = query_head_norm[:, PROMPT_LENGTH:].reshape(slot_total_count, RESPONSE_LENGTH, KEY_VALUE_HEADS, query_group_size, HEAD_SIZE)
    response_keys = key_head_norm[:, PROMPT_LENGTH:].reshape(slot_total_count, RESPONSE_LENGTH, KEY_VALUE_HEADS, HEAD_SIZE)
    response_values = value_row_block[:, PROMPT_LENGTH:].reshape(slot_total_count, RESPONSE_LENGTH, KEY_VALUE_HEADS, HEAD_SIZE)
    response_output_gradient = gradient_rows[:, PROMPT_LENGTH:].reshape(slot_total_count, RESPONSE_LENGTH, KEY_VALUE_HEADS, query_group_size, HEAD_SIZE)

    def reply_step(carried, inputs):
        key_accumulator, value_accumulator = carried
        q_rows, k_rows, v_rows, d_rows, owner = inputs
        prompt_keys = lax.dynamic_index_in_dim(key_head_norm, owner, 0, keepdims=False)[:PROMPT_LENGTH]
        prompt_values = lax.dynamic_index_in_dim(value_row_block, owner, 0, keepdims=False)[:PROMPT_LENGTH]
        length = lax.dynamic_index_in_dim(prompt_len, owner, 0, keepdims=False)
        visible = jnp.concatenate([jnp.broadcast_to(jnp.arange(PROMPT_LENGTH)[None, :] < length, (RESPONSE_LENGTH, PROMPT_LENGTH)), own_part], axis=1)
        q_grad, k_grad, v_grad = per_head(q_rows, jnp.concatenate([prompt_keys, k_rows], axis=0), jnp.concatenate([prompt_values, v_rows], axis=0), d_rows, visible)
        key_accumulator = key_accumulator.at[owner].add(k_grad[:PROMPT_LENGTH])
        value_accumulator = value_accumulator.at[owner].add(v_grad[:PROMPT_LENGTH])
        return ((key_accumulator, value_accumulator), (q_grad, k_grad[PROMPT_LENGTH:], v_grad[PROMPT_LENGTH:]))
    start_offset = jnp.zeros((N_DP, PROMPT_LENGTH, KEY_VALUE_HEADS, HEAD_SIZE), jnp.float32)
    (key_accumulator, value_accumulator), (response_query_gradient, response_key_gradient, response_value_gradient) = lax.scan(reply_step, (start_offset, start_offset), (response_queries, response_keys, response_values, response_output_gradient, resp_owner))
    key_row_block = jnp.concatenate([prompt_key_gradient + key_accumulator, response_key_gradient.reshape(N_DP, RESPONSE_SLOTS * RESPONSE_LENGTH, KEY_VALUE_HEADS, HEAD_SIZE)], axis=1)
    value_running_sums = jnp.concatenate([prompt_value_gradient + value_accumulator, response_value_gradient.reshape(N_DP, RESPONSE_SLOTS * RESPONSE_LENGTH, KEY_VALUE_HEADS, HEAD_SIZE)], axis=1)
    query_row_block = jnp.concatenate([prompt_query_gradient, response_query_gradient.reshape(N_DP, RESPONSE_SLOTS * RESPONSE_LENGTH, KEY_VALUE_HEADS, query_group_size, HEAD_SIZE)], axis=1)
    query_backward, query_portion = norm_backward(query_row_block, query_unnormed, query_inv, q_gain)
    key_backward, key_portion = norm_backward(key_row_block, key_unnormed, key_inv, k_gain)
    overall_rows = N_DP * row_total_count
    return (query_backward.reshape(overall_rows, QUERY_HEADS * HEAD_SIZE).astype(jnp.bfloat16), key_backward.reshape(overall_rows, KEY_VALUE_HEADS * HEAD_SIZE).astype(jnp.bfloat16), value_running_sums.reshape(overall_rows, KEY_VALUE_HEADS * HEAD_SIZE).astype(jnp.bfloat16), query_portion, key_portion)
```

```python
import functools

import jax
import jax.numpy as jnp
from jax import lax
from jax.experimental import pallas as pl
from jax.experimental.pallas import tpu as pltpu
from jax.sharding import PartitionSpec as P

PROMPT = 256
RESP = 64
HEAD = 128
KEYS = PROMPT + RESP
EPSILON = 1e-06
SCALE = HEAD ** (-0.5)
LOG2E = 1.4426950408889634
SHARP = SCALE * LOG2E
MASKED = -1e30
MESH = pl.DeviceIdType.MESH
F32 = jnp.float32
BF16 = jnp.bfloat16
NT = (((1,), (1,)), ((), ()))


def dot_nn(a, b):
    return jnp.dot(a, b, preferred_element_type=F32)


def dot_nt(a, b):
    return lax.dot_general(a, b, NT, preferred_element_type=F32)


def normed_rows(rows):
    wide = rows.astype(F32)
    inverse = lax.rsqrt(jnp.mean(wide * wide, axis=1, keepdims=True) + EPSILON)
    return wide, inverse


def softmax_columns(blocks, keep):
    top = functools.reduce(jnp.maximum, [jnp.max(b, axis=0, keepdims=True) for b in blocks])
    shift = top * SHARP
    raised = [jnp.exp2(b * SHARP - shift) for b in blocks]
    total = functools.reduce(jnp.add, [jnp.sum(b, axis=0, keepdims=True) for b in raised])
    factor = keep / total
    return [b * factor for b in raised]


def score_gradient(probs, weights, p_grads):
    inner = functools.reduce(
        jnp.add,
        [
            jnp.sum(w.astype(F32) * g, axis=0, keepdims=True)
            for w, g in zip(weights, p_grads, strict=True)
        ],
    )
    return [(p * (g - inner)).astype(BF16) for p, g in zip(probs, p_grads, strict=True)]


def kernel(
    heads,
    groups,
    n_dp,
    n_tensor,
    plen,
    rlen,
    rown,
    qg,
    kg,
    q_hbm,
    k_hbm,
    v_hbm,
    o_hbm,
    dq_hbm,
    dk_out,
    dv_out,
    qg_out,
    kg_out,
    qv,
    ov,
    dqv,
    kself,
    vself,
    near_k0,
    near_k1,
    near_v0,
    near_v1,
    eye,
    gain_col,
    bias_p,
    bias_own,
    kn_p,
    knt_p,
    dk_acc,
    dv_acc,
    qg_acc,
    kg_acc,
    r_o,
    r_qt,
    r_qnt,
    r_inv,
    r_k,
    r_kt,
    r_khat,
    r_p,
    r_v,
    r_dv,
    r_dk,
    back,
    back_sib,
    back_r4,
    back_r2,
    back_o4,
    back_o2,
    part_a,
    part_b,
    buf_a,
    buf_b,
    load_sem,
    store_sem,
    fwd_send,
    fwd_recv,
    bwd_send,
    bwd_recv,
    a_send,
    a_recv,
    b_send,
    b_recv,
):
    dp = lax.axis_index("dp")
    tensor = lax.axis_index("tensor")
    core = lax.rem(dp, 2)
    up = (lax.rem(dp + 2, n_dp), tensor)
    down = (lax.rem(dp + n_dp - 2, n_dp), tensor)
    sibling = (dp + 1 - 2 * core, tensor)
    near = (near_k0, near_k1, near_v0, near_v1)
    chunks = 2 * heads

    columns = n_dp // 16
    n_a = columns * n_tensor
    place_a = lax.div(dp, 16) * n_tensor + tensor
    place_b = lax.rem(dp, 16)

    def peer_a(k):
        place = lax.rem(place_a + k, n_a)
        return place, (lax.div(place, n_tensor) * 16 + place_b, lax.rem(place, n_tensor))

    def peer_b(k):
        place = lax.rem(place_b + k, 16)
        return place, (dp - place_b + place, tensor)

    def cols(h, g=None):
        if g is None:
            return pl.ds(h * HEAD, HEAD)
        return pl.ds(pl.multiple_of((h * groups + g) * HEAD, HEAD), HEAD)

    loads = []

    def load(src, dst):
        copy = pltpu.make_async_copy(src, dst, load_sem.at[len(loads)])
        copy.start()
        loads.append(copy)
        return copy

    staged = []
    for c in range(chunks):
        h = c % heads
        source = (k_hbm if c < heads else v_hbm).at[pl.ds(0, PROMPT), cols(h)]
        staged.append(load(source, near[c].at[0, pl.ds(0, PROMPT)]))
    load_k = load(k_hbm, kself)
    wide = groups * HEAD
    load_q, load_o = [], []
    for h in range(heads):
        load_q.append(load(q_hbm.at[:, pl.ds(h * wide, wide)], qv.at[:, pl.ds(h * wide, wide)]))
        load_o.append(load(o_hbm.at[:, pl.ds(h * wide, wide)], ov.at[:, pl.ds(h * wide, wide)]))
        if h == 0:
            load_v = load(v_hbm, vself)

    barrier = pltpu.get_barrier_semaphore()
    for neighbour in (up, down):
        pl.semaphore_signal(barrier, inc=1, device_id=neighbour, device_id_type=MESH)

    @pl.loop(1, 16)
    def _(k):
        pl.semaphore_signal(barrier, inc=1, device_id=peer_b(k)[1], device_id_type=MESH)

    if n_a > 1:

        @pl.loop(1, n_a)
        def _(k):
            pl.semaphore_signal(barrier, inc=1, device_id=peer_a(k)[1], device_id_type=MESH)

    row_at = lax.broadcasted_iota(jnp.int32, (HEAD, HEAD), 0)
    col_at = lax.broadcasted_iota(jnp.int32, (HEAD, HEAD), 1)
    eye[...] = jnp.where(row_at == col_at, 1.0, 0.0).astype(BF16)
    gain_col[...] = jnp.broadcast_to(qg[...], (HEAD, HEAD)).T
    length = plen[0]
    key_at = lax.broadcasted_iota(jnp.int32, (PROMPT, PROMPT), 0)
    query_at = lax.broadcasted_iota(jnp.int32, (PROMPT, PROMPT), 1)
    bias_p[...] = jnp.where((key_at <= query_at) & (key_at < length), 0.0, MASKED)
    own_key = lax.broadcasted_iota(jnp.int32, (RESP, HEAD), 0)
    own_query = lax.rem(lax.broadcasted_iota(jnp.int32, (RESP, HEAD), 1), RESP)
    bias_own[...] = jnp.where(own_key <= own_query, 0.0, MASKED)
    near_k0[0, pl.ds(PROMPT, 16)] = jnp.full((16, HEAD), length.astype(F32)).astype(BF16)
    qg_acc[...] = jnp.zeros_like(qg_acc)
    kg_acc[...] = jnp.zeros_like(kg_acc)
    dk_acc[...] = jnp.zeros_like(dk_acc)
    dv_acc[...] = jnp.zeros_like(dv_acc)
    keep_p = (lax.broadcasted_iota(jnp.int32, (1, PROMPT), 1) < length).astype(F32)
    picks = [lax.rem(dp + n_dp - rown[s], n_dp) for s in range(2)]

    for copy in staged:
        copy.wait()
    pl.semaphore_wait(barrier, 2 + 15 + n_a - 1)

    def slot(c, d):
        return near[c].at[d]

    def forward(kind, c, src, dst, device):
        return pltpu.make_async_remote_copy(
            src_ref=slot(c, src),
            dst_ref=slot(c, dst),
            send_sem=fwd_send.at[kind, c],
            recv_sem=fwd_recv.at[kind, c],
            device_id=device,
            device_id_type=MESH,
        )

    def hop(c):
        return forward(0, c, 0, 2, up)

    def relay(c):
        return forward(1, c, 2, 4, up)

    def across(c, far, src):
        return forward(2 + far, c, src, 1 + 2 * far, sibling)

    def send_own(c):
        hop(c).start()

        @pl.when(core == 0)
        def _():
            across(c, 0, 0).start()

    def pass_on(c):
        hop(c).wait_recv()
        relay(c).start()

        @pl.when(core == 0)
        def _():
            across(c, 1, 2).start()

        @pl.when(core == 1)
        def _():
            across(c, 0, 2).start()

    def arrive(c):
        relay(c).wait_recv()

        @pl.when(core == 1)
        def _():
            across(c, 1, 4).start()

        across(c, 0, 0).wait_recv()
        across(c, 1, 0).wait_recv()

    def prepared(rows):
        qt = dot_nt(eye[...], rows)
        inverse = lax.rsqrt(jnp.mean(qt * qt, axis=0, keepdims=True) + EPSILON)
        gain = jnp.concatenate([gain_col[...]] * (qt.shape[1] // HEAD), axis=1)
        return qt, inverse, (qt * inverse * gain).astype(BF16)

    def query_backward(grad, qt, inverse):
        gain = jnp.concatenate([gain_col[...]] * (qt.shape[1] // HEAD), axis=1)
        both = grad * qt
        mean = jnp.mean(both * gain, axis=0, keepdims=True)
        scaled = inverse * SCALE
        out = grad * gain * scaled - qt * (inverse * inverse * scaled * mean)
        portion = both * scaled
        for at in range(0, qt.shape[1], HEAD):
            qg_acc[...] += portion[:, at : at + HEAD]
        return out.T.astype(BF16)

    def prepare_prompt_keys(h):
        wide_k, inverse = normed_rows(kself[pl.ds(0, PROMPT), cols(h)])
        normed = (wide_k * inverse * kg[...]).astype(BF16)
        kn_p[h] = normed
        knt_p[h] = dot_nt(eye[...], normed).astype(BF16)

    def prompt_unit(h, g):
        at = cols(h, g)
        qt, inverse, qnt = prepared(qv[pl.ds(0, PROMPT), at])
        rows_o = ov[pl.ds(0, PROMPT), at]
        scores = dot_nn(kn_p[h], qnt)
        p_grad = dot_nt(vself[pl.ds(0, PROMPT), cols(h)], rows_o)
        half = PROMPT // 2
        left = [scores[:half, :half] + bias_p[:half, :half]]
        right = [
            scores[:half, half:] + bias_p[:half, half:],
            scores[half:, half:] + bias_p[half:, half:],
        ]
        left_p = softmax_columns(left, keep_p[:, :half])
        right_p = softmax_columns(right, keep_p[:, half:])
        left_w = [p.astype(BF16) for p in left_p]
        right_w = [p.astype(BF16) for p in right_p]
        left_s = score_gradient(left_p, left_w, [p_grad[:half, :half]])
        right_s = score_gradient(right_p, right_w, [p_grad[:half, half:], p_grad[half:, half:]])
        empty = jnp.zeros((half, half), BF16)

        def square(a, b):
            return jnp.concatenate(
                [jnp.concatenate([a[0], empty], axis=0), jnp.concatenate(b, axis=0)], axis=1
            )

        weights = square(left_w, right_w)
        s_grad = square(left_s, right_s)
        dv_acc[h] += dot_nn(weights, rows_o)
        dk_acc[h] += dot_nt(s_grad, qnt)
        grad = dot_nn(knt_p[h], s_grad)
        dqv[pl.ds(0, PROMPT), at] = query_backward(grad, qt, inverse)

    def prompt_units(h, first, last):
        @pl.loop(first, last)
        def _(g):
            prompt_unit(h, g)

    def response_rows(s):
        return pl.ds(pl.multiple_of(PROMPT + s * RESP, RESP), RESP)

    def prepare_responses(h):
        @pl.loop(0, 2)
        def _(s):
            rows = response_rows(s)
            stacked = jnp.concatenate([qv[rows, cols(h, g)] for g in range(groups)], axis=0)
            r_o[h, s] = jnp.concatenate([ov[rows, cols(h, g)] for g in range(groups)], axis=0)
            qt, inverse, qnt = prepared(stacked)
            r_qt[h, s] = qt
            r_qnt[h, s] = qnt
            r_inv[h, s] = jnp.broadcast_to(inverse, (8, inverse.shape[1]))

    span = 2 * HEAD

    def response_keys(h):
        @pl.loop(0, 2)
        def _(s):
            pick = jnp.clip(lax.rem(dp + n_dp - rown[s], n_dp), 1, 4)
            rows = response_rows(s)
            wide_k, inverse = normed_rows(near[h][pick, pl.ds(0, PROMPT)])
            hat = wide_k * inverse
            r_khat[h, s, pl.ds(0, PROMPT)] = hat
            r_k[h, s, pl.ds(0, PROMPT)] = (hat * kg[...]).astype(BF16)
            wide_k, inverse = normed_rows(kself[rows, cols(h)])
            hat = wide_k * inverse
            r_khat[h, s, pl.ds(PROMPT, RESP)] = hat
            r_k[h, s, pl.ds(PROMPT, RESP)] = (hat * kg[...]).astype(BF16)
            normed = r_k[h, s]
            r_kt[h, s] = dot_nt(eye[...], normed).astype(BF16)
            owner_length = near_k0[pick, pl.ds(PROMPT, 16)].astype(F32)[0:1]
            at = lax.broadcasted_iota(jnp.int32, (PROMPT, HEAD), 0).astype(F32)
            bias = jnp.where(at < owner_length, 0.0, MASKED)
            bias = jnp.concatenate([bias, bias_own[...]], axis=0)
            bias = jnp.concatenate([bias, bias], axis=1)
            place = lax.rem(lax.broadcasted_iota(jnp.int32, (1, span), 1), RESP)
            keep = (place < rlen[s]).astype(F32)
            total = jnp.zeros((KEYS, HEAD), F32)
            for first in range(0, groups * RESP, span):
                block = pl.ds(first, span)
                scores = dot_nn(normed, r_qnt[h, s, :, block]) + bias
                (probs,) = softmax_columns([scores], keep)
                r_p[h, s, :, block] = probs
                total = total + dot_nn(probs.astype(BF16), r_o[h, s, block])
            r_dv[h, s] = total

    def response_values(h):
        @pl.loop(0, 2)
        def _(s):
            pick = jnp.clip(lax.rem(dp + n_dp - rown[s], n_dp), 1, 4)
            rows = response_rows(s)
            r_v[pl.ds(0, PROMPT)] = near[heads + h][pick]
            r_v[pl.ds(PROMPT, RESP)] = vself[rows, cols(h)]
            total = jnp.zeros((KEYS, HEAD), F32)
            for first in range(0, groups * RESP, span):
                block = pl.ds(first, span)
                probs = r_p[h, s, :, block]
                p_grad = dot_nt(r_v[...], r_o[h, s, block])
                (s_grad,) = score_gradient([probs], [probs.astype(BF16)], [p_grad])
                total = total + dot_nt(s_grad, r_qnt[h, s, :, block])
                grad = dot_nn(r_kt[h, s], s_grad)
                out = query_backward(grad, r_qt[h, s, :, block], r_inv[h, s, 0:1, block])
                for i in range(span // RESP):
                    dqv[rows, cols(h, first // RESP + i)] = out[i * RESP : (i + 1) * RESP]
            r_dk[h, s] = total
            portion = total * r_khat[h, s] * SCALE
            kg_acc[...] += jnp.sum(portion.reshape(KEYS // 8, 8, HEAD), axis=0)

    def key_backward(grad, rows):
        wide_k, inverse = normed_rows(rows)
        scaled = grad * kg[...]
        mean = jnp.mean(scaled * wide_k, axis=1, keepdims=True)
        factor = inverse * SCALE
        return (scaled * factor - wide_k * (inverse * inverse * factor * mean)).astype(BF16)

    def backward(kind, c, src, dst, device):
        return pltpu.make_async_remote_copy(
            src_ref=src,
            dst_ref=dst,
            send_sem=bwd_send.at[kind, c],
            recv_sem=bwd_recv.at[kind, c],
            device_id=device,
            device_id_type=MESH,
        )

    def back_across(c):
        return backward(0, c, back.at[c, pl.ds(0, 2)], back_sib.at[c], sibling)

    def back_far(c):
        return backward(1, c, back_o4.at[c], back_r4.at[c], down)

    def back_near(c):
        return backward(2, c, back_o2.at[c], back_r2.at[c], down)

    def give_back(c, terms):
        for i, distance in enumerate((1, 3, 2, 4)):
            first = (picks[0] == distance).astype(F32)
            second = (picks[1] == distance).astype(F32)
            term = first * terms[0, pl.ds(0, PROMPT)] + second * terms[1, pl.ds(0, PROMPT)]
            back[c, i] = term.astype(BF16)
        back_across(c).start()

    upper = core.astype(F32)

    def give_back_far(c):
        back_across(c).wait_recv()
        total = back[c, 3].astype(F32) + upper * back_sib[c, 1].astype(F32)
        back_o4[c] = total.astype(BF16)
        back_far(c).start()

    def give_back_near(c):
        back_far(c).wait_recv()
        other = upper * back_sib[c, 0].astype(F32) + (1.0 - upper) * back_sib[c, 1].astype(F32)
        total = back[c, 2].astype(F32) + back_r4[c].astype(F32) + other
        back_o2[c] = total.astype(BF16)
        back_near(c).start()

    def taken_back(c):
        back_near(c).wait_recv()
        return back_r2[c].astype(F32) + (1.0 - upper) * back_sib[c, 0].astype(F32)

    def exchange(n, peer, place, source, buffer, send_sem, recv_sem):
        def copy(k):
            other, device = peer(k)
            return pltpu.make_async_remote_copy(
                src_ref=source,
                dst_ref=buffer.at[place],
                send_sem=send_sem.at[other],
                recv_sem=recv_sem.at[place],
                device_id=device,
                device_id_type=MESH,
            )

        def arriving(k):
            other, device = peer(k)
            return pltpu.make_async_remote_copy(
                src_ref=source,
                dst_ref=buffer.at[other],
                send_sem=send_sem.at[other],
                recv_sem=recv_sem.at[other],
                device_id=device,
                device_id_type=MESH,
            )

        def start():
            if n > 1:

                @pl.loop(1, n)
                def _(k):
                    copy(k).start()

        def collect():
            buffer[place] = source[...]
            if n > 1:

                @pl.loop(1, n)
                def _(k):
                    arriving(k).wait_recv()

            total = buffer[0]
            for i in range(1, n):
                total = total + buffer[i]
            return total

        def finish():
            if n > 1:

                @pl.loop(1, n)
                def _(k):
                    copy(k).wait_send()

        return start, collect, finish

    start_a, collect_a, finish_a = exchange(n_a, peer_a, place_a, part_a, buf_a, a_send, a_recv)
    start_b, collect_b, finish_b = exchange(16, peer_b, place_b, part_b, buf_b, b_send, b_recv)

    for c in range(chunks):
        send_own(c)
    load_k.wait()
    load_v.wait()
    load_q[0].wait()
    load_o[0].wait()
    prepare_prompt_keys(0)
    prompt_units(0, 0, groups)
    load_q[1].wait()
    load_o[1].wait()
    prepare_prompt_keys(1)
    pass_on(0)
    prepare_responses(0)
    prepare_responses(1)
    pass_on(1)
    prompt_units(1, 0, 3)
    pass_on(2)
    prompt_units(1, 3, 6)
    pass_on(3)
    prompt_units(1, 6, groups)
    stores = [
        pltpu.make_async_copy(
            dqv.at[pl.ds(0, PROMPT)], dq_hbm.at[pl.ds(0, PROMPT)], store_sem.at[0]
        )
    ]
    stores[0].start()
    for h in range(heads):
        portion = jnp.zeros((8, HEAD), F32)
        wide_k, inverse = normed_rows(kself[pl.ds(0, PROMPT), cols(h)])
        portion = dk_acc[h] * (wide_k * inverse) * SCALE
        kg_acc[...] += jnp.sum(portion.reshape(PROMPT // 8, 8, HEAD), axis=0)

    arrive(0)
    response_keys(0)
    give_back(2, r_dv.at[0])
    arrive(1)
    response_keys(1)
    give_back(3, r_dv.at[1])
    give_back_far(2)
    arrive(2)
    response_values(0)
    give_back(0, r_dk.at[0])
    give_back_far(3)
    arrive(3)
    response_values(1)
    give_back(1, r_dk.at[1])
    part_a[...] = jnp.concatenate(
        [
            jnp.sum(qg_acc[...].T, axis=0, keepdims=True),
            jnp.sum(kg_acc[...], axis=0, keepdims=True),
            jnp.zeros((6, HEAD), F32),
        ],
        axis=0,
    )
    start_a()
    give_back_far(0)
    give_back_far(1)
    stores.append(
        pltpu.make_async_copy(
            dqv.at[pl.ds(PROMPT, 2 * RESP)], dq_hbm.at[pl.ds(PROMPT, 2 * RESP)], store_sem.at[1]
        )
    )
    stores[1].start()
    give_back_near(2)
    give_back_near(3)
    give_back_near(0)
    for h in range(heads):
        for s in range(2):
            rows = pl.ds(PROMPT + s * RESP, RESP)
            dv_out[rows, cols(h)] = r_dv[h, s, pl.ds(PROMPT, RESP)].astype(BF16)
            dk_out[rows, cols(h)] = key_backward(
                r_dk[h, s, pl.ds(PROMPT, RESP)], kself[rows, cols(h)]
            )
    part_b[...] = collect_a()
    start_b()
    give_back_near(1)
    prompt = pl.ds(0, PROMPT)
    for h in range(heads):
        dv_out[prompt, cols(h)] = (dv_acc[h] + taken_back(heads + h)).astype(BF16)
    for h in range(heads):
        dk_out[prompt, cols(h)] = key_backward(
            dk_acc[h] + taken_back(h), kself[prompt, cols(h)]
        )
    sums = collect_b()
    qg_out[...] = sums[0:1]
    kg_out[...] = sums[1:2]

    finish_a()
    finish_b()
    for c in range(chunks):
        hop(c).wait_send()
        relay(c).wait_send()
        across(c, 0, 0).wait_send()
        across(c, 1, 0).wait_send()
        back_across(c).wait_send()
        back_far(c).wait_send()
        back_near(c).wait_send()
    for copy in stores:
        copy.wait()


def on_device(
    n_dp, n_tensor, queries, keys, values, output_gradient, q_gain, k_gain, prompt_len, resp_len, resp_owner
):
    heads = keys.shape[1] // HEAD
    groups = queries.shape[1] // keys.shape[1]
    rows = queries.shape[0]
    chunks = 2 * heads
    n_a = n_dp // 16 * n_tensor
    vmem = pl.BlockSpec(memory_space=pltpu.VMEM)
    smem = pl.BlockSpec(memory_space=pltpu.SMEM)
    hbm = pl.BlockSpec(memory_space=pltpu.HBM)
    asked = groups * RESP
    scratch = [
        pltpu.VMEM(queries.shape, BF16),
        pltpu.VMEM(queries.shape, BF16),
        pltpu.VMEM(queries.shape, BF16),
        pltpu.VMEM(keys.shape, BF16),
        pltpu.VMEM(keys.shape, BF16),
        pltpu.VMEM((5, PROMPT + 16, HEAD), BF16),
        pltpu.VMEM((5, PROMPT, HEAD), BF16),
        pltpu.VMEM((5, PROMPT, HEAD), BF16),
        pltpu.VMEM((5, PROMPT, HEAD), BF16),
        pltpu.VMEM((HEAD, HEAD), BF16),
        pltpu.VMEM((HEAD, HEAD), F32),
        pltpu.VMEM((PROMPT, PROMPT), F32),
        pltpu.VMEM((RESP, HEAD), F32),
        pltpu.VMEM((heads, PROMPT, HEAD), BF16),
        pltpu.VMEM((heads, HEAD, PROMPT), BF16),
        pltpu.VMEM((heads, PROMPT, HEAD), F32),
        pltpu.VMEM((heads, PROMPT, HEAD), F32),
        pltpu.VMEM((HEAD, HEAD), F32),
        pltpu.VMEM((8, HEAD), F32),
        pltpu.VMEM((heads, 2, asked, HEAD), BF16),
        pltpu.VMEM((heads, 2, HEAD, asked), F32),
        pltpu.VMEM((heads, 2, HEAD, asked), BF16),
        pltpu.VMEM((heads, 2, 8, asked), F32),
        pltpu.VMEM((heads, 2, KEYS, HEAD), BF16),
        pltpu.VMEM((heads, 2, HEAD, KEYS), BF16),
        pltpu.VMEM((heads, 2, KEYS, HEAD), F32),
        pltpu.VMEM((heads, 2, KEYS, asked), F32),
        pltpu.VMEM((KEYS, HEAD), BF16),
        pltpu.VMEM((heads, 2, KEYS, HEAD), F32),
        pltpu.VMEM((heads, 2, KEYS, HEAD), F32),
        pltpu.VMEM((chunks, 4, PROMPT, HEAD), BF16),
        pltpu.VMEM((chunks, 2, PROMPT, HEAD), BF16),
        pltpu.VMEM((chunks, PROMPT, HEAD), BF16),
        pltpu.VMEM((chunks, PROMPT, HEAD), BF16),
        pltpu.VMEM((chunks, PROMPT, HEAD), BF16),
        pltpu.VMEM((chunks, PROMPT, HEAD), BF16),
        pltpu.VMEM((8, HEAD), F32),
        pltpu.VMEM((8, HEAD), F32),
        pltpu.VMEM((n_a, 8, HEAD), F32),
        pltpu.VMEM((16, 8, HEAD), F32),
        pltpu.SemaphoreType.DMA((chunks + 2 + 2 * heads,)),
        pltpu.SemaphoreType.DMA((2,)),
        pltpu.SemaphoreType.DMA((4, chunks)),
        pltpu.SemaphoreType.DMA((4, chunks)),
        pltpu.SemaphoreType.DMA((3, chunks)),
        pltpu.SemaphoreType.DMA((3, chunks)),
        pltpu.SemaphoreType.DMA((n_a,)),
        pltpu.SemaphoreType.DMA((n_a,)),
        pltpu.SemaphoreType.DMA((16,)),
        pltpu.SemaphoreType.DMA((16,)),
    ]
    q_grad, k_grad, v_grad, q_gain_grad, k_gain_grad = pl.pallas_call(
        functools.partial(kernel, heads, groups, n_dp, n_tensor),
        out_shape=(
            jax.ShapeDtypeStruct(queries.shape, BF16),
            jax.ShapeDtypeStruct(keys.shape, BF16),
            jax.ShapeDtypeStruct(keys.shape, BF16),
            jax.ShapeDtypeStruct((1, HEAD), F32),
            jax.ShapeDtypeStruct((1, HEAD), F32),
        ),
        in_specs=[smem, smem, smem, vmem, vmem, hbm, hbm, hbm, hbm],
        out_specs=(hbm, vmem, vmem, vmem, vmem),
        scratch_shapes=scratch,
        compiler_params=pltpu.CompilerParams(
            collective_id=0, has_side_effects=True, vmem_limit_bytes=56 * 2**20
        ),
        name="attention",
    )(
        prompt_len,
        resp_len,
        resp_owner,
        q_gain.reshape(1, HEAD),
        k_gain.reshape(1, HEAD),
        queries,
        keys,
        values,
        output_gradient,
    )
    return q_grad, k_grad, v_grad, q_gain_grad.reshape(HEAD), k_gain_grad.reshape(HEAD)


def solution(mesh):
    rows, whole = P("dp", "tensor"), P()
    return jax.shard_map(
        functools.partial(on_device, mesh.shape["dp"], mesh.shape["tensor"]),
        mesh=mesh,
        in_specs=(rows, rows, rows, rows, whole, whole, P("dp"), P("dp"), P("dp")),
        out_specs=(rows, rows, rows, whole, whole),
        check_vma=False,
    )
```

```python
import functools

import jax
import jax.numpy as jnp
from jax import lax
from jax.experimental import pallas as pl
from jax.experimental.pallas import tpu as pltpu
from jax.sharding import PartitionSpec as P

PROMPT = 256
RESP = 64
HEAD = 128
KEYS = PROMPT + RESP
EPSILON = 1e-06
SCALE = HEAD ** (-0.5)
LOG2E = 1.4426950408889634
SHARP = SCALE * LOG2E
MASKED = -1e30
MESH = pl.DeviceIdType.MESH
F32 = jnp.float32
BF16 = jnp.bfloat16
NT = (((1,), (1,)), ((), ()))


def dot_nn(a, b):
    return jnp.dot(a, b, preferred_element_type=F32)


def dot_nt(a, b):
    return lax.dot_general(a, b, NT, preferred_element_type=F32)


def normed_rows(rows):
    wide = rows.astype(F32)
    inverse = lax.rsqrt(jnp.mean(wide * wide, axis=1, keepdims=True) + EPSILON)
    return wide, inverse


def softmax_columns(blocks, keep):
    top = functools.reduce(jnp.maximum, [jnp.max(b, axis=0, keepdims=True) for b in blocks])
    shift = top * SHARP
    raised = [jnp.exp2(b * SHARP - shift) for b in blocks]
    total = functools.reduce(jnp.add, [jnp.sum(b, axis=0, keepdims=True) for b in raised])
    factor = keep / total
    return [b * factor for b in raised]


def score_gradient(probs, weights, p_grads):
    inner = functools.reduce(
        jnp.add,
        [
            jnp.sum(w.astype(F32) * g, axis=0, keepdims=True)
            for w, g in zip(weights, p_grads, strict=True)
        ],
    )
    return [(p * (g - inner)).astype(BF16) for p, g in zip(probs, p_grads, strict=True)]


def kernel(
    heads,
    groups,
    n_dp,
    n_tensor,
    plen,
    rlen,
    rown,
    qg,
    kg,
    q_hbm,
    k_hbm,
    v_hbm,
    o_hbm,
    dqv,
    dk_out,
    dv_out,
    gains_out,
    qv,
    ov,
    kself,
    vself,
    near_k0,
    near_k1,
    near_v0,
    near_v1,
    eye,
    gain_col,
    bias_lower,
    bias_upper,
    bias_own,
    kn_p,
    knt_p,
    dk_acc,
    dv_acc,
    qg_acc,
    kg_acc,
    r_o,
    r_qt,
    r_qnt,
    r_inv,
    r_k,
    r_kt,
    r_khat,
    r_p,
    back,
    back_sib,
    back_r4,
    back_r2,
    back_o4,
    back_o2,
    part_a,
    part_b,
    buf_a,
    buf_b,
    load_sem,
    fwd_send,
    fwd_recv,
    bwd_send,
    bwd_recv,
    a_send,
    a_recv,
    b_send,
    b_recv,
):
    dp = lax.axis_index("dp")
    tensor = lax.axis_index("tensor")
    core = lax.rem(dp, 2)
    up = (lax.rem(dp + 2, n_dp), tensor)
    down = (lax.rem(dp + n_dp - 2, n_dp), tensor)
    sibling = (dp + 1 - 2 * core, tensor)
    near = (near_k0, near_k1, near_v0, near_v1)
    chunks = 2 * heads

    columns = n_dp // 16
    n_a = columns * n_tensor
    place_a = lax.div(dp, 16) * n_tensor + tensor
    place_b = lax.rem(dp, 16)

    def peer_a(k):
        place = lax.rem(place_a + k, n_a)
        return place, (lax.div(place, n_tensor) * 16 + place_b, lax.rem(place, n_tensor))

    def peer_b(k):
        place = lax.rem(place_b + k, 16)
        return place, (dp - place_b + place, tensor)

    def cols(h, g=None):
        if g is None:
            return pl.ds(h * HEAD, HEAD)
        return pl.ds(pl.multiple_of((h * groups + g) * HEAD, HEAD), HEAD)

    loads = []

    def load(src, dst):
        copy = pltpu.make_async_copy(src, dst, load_sem.at[len(loads)])
        copy.start()
        loads.append(copy)
        return copy

    staged = []
    for c in range(chunks):
        h = c % heads
        source = (k_hbm if c < heads else v_hbm).at[pl.ds(0, PROMPT), cols(h)]
        staged.append(load(source, near[c].at[0, pl.ds(0, PROMPT)]))
    load_k = load(k_hbm, kself)
    wide = groups * HEAD
    load_q, load_o = [], []
    for h in range(heads):
        load_q.append(load(q_hbm.at[:, pl.ds(h * wide, wide)], qv.at[:, pl.ds(h * wide, wide)]))
        load_o.append(load(o_hbm.at[:, pl.ds(h * wide, wide)], ov.at[:, pl.ds(h * wide, wide)]))
        if h == 0:
            load_v = load(v_hbm, vself)

    barrier = pltpu.get_barrier_semaphore()
    for neighbour in (up, down):
        pl.semaphore_signal(barrier, inc=1, device_id=neighbour, device_id_type=MESH)

    @pl.loop(1, 16)
    def _(k):
        pl.semaphore_signal(barrier, inc=1, device_id=peer_b(k)[1], device_id_type=MESH)

    if n_a > 1:

        @pl.loop(1, n_a)
        def _(k):
            pl.semaphore_signal(barrier, inc=1, device_id=peer_a(k)[1], device_id_type=MESH)

    length = plen[0]
    query_at = lax.rem(lax.broadcasted_iota(jnp.int32, (1, PROMPT), 1), PROMPT // 2)
    keep_lower = (query_at < length).astype(F32)
    keep_upper = (query_at + PROMPT // 2 < length).astype(F32)
    near_k0[0, pl.ds(PROMPT, 16)] = jnp.full((16, HEAD), length.astype(F32)).astype(BF16)

    def prepare():
        row_at = lax.broadcasted_iota(jnp.int32, (HEAD, HEAD), 0)
        col_at = lax.broadcasted_iota(jnp.int32, (HEAD, HEAD), 1)
        eye[...] = jnp.where(row_at == col_at, 1.0, 0.0).astype(BF16)
        gain_col[...] = jnp.broadcast_to(qg[...], (HEAD, HEAD)).T
        for lower, bias in ((True, bias_lower), (False, bias_upper)):
            key_at = lax.broadcasted_iota(jnp.int32, bias.shape, 0)
            query_at = lax.rem(lax.broadcasted_iota(jnp.int32, bias.shape, 1), PROMPT // 2)
            query_at = query_at if lower else query_at + PROMPT // 2
            bias[...] = jnp.where((key_at <= query_at) & (key_at < length), 0.0, MASKED)
        own_key = lax.broadcasted_iota(jnp.int32, (RESP, HEAD), 0)
        own_query = lax.rem(lax.broadcasted_iota(jnp.int32, (RESP, HEAD), 1), RESP)
        bias_own[...] = jnp.where(own_key <= own_query, 0.0, MASKED)
        qg_acc[...] = jnp.zeros_like(qg_acc)
        kg_acc[...] = jnp.zeros_like(kg_acc)
        dk_acc[...] = jnp.zeros_like(dk_acc)
        dv_acc[...] = jnp.zeros_like(dv_acc)

    picks = [jnp.clip(lax.rem(dp + n_dp - rown[s], n_dp), 1, 4) for s in range(2)]

    for copy in staged:
        copy.wait()
    pl.semaphore_wait(barrier, 2 + 15 + n_a - 1)

    def slot(c, d):
        return near[c].at[d]

    def forward(kind, c, src, dst, device):
        return pltpu.make_async_remote_copy(
            src_ref=slot(c, src),
            dst_ref=slot(c, dst),
            send_sem=fwd_send.at[kind, c],
            recv_sem=fwd_recv.at[kind, c],
            device_id=device,
            device_id_type=MESH,
        )

    def hop(c):
        return forward(0, c, 0, 2, up)

    def relay(c):
        return forward(1, c, 2, 4, up)

    def across(c, far, src):
        return forward(2 + far, c, src, 1 + 2 * far, sibling)

    def send_own(c):
        hop(c).start()

        @pl.when(core == 0)
        def _():
            across(c, 0, 0).start()

    def pass_on(c):
        hop(c).wait_recv()
        relay(c).start()

        @pl.when(core == 0)
        def _():
            across(c, 1, 2).start()

        @pl.when(core == 1)
        def _():
            across(c, 0, 2).start()

    def arrive(c):
        relay(c).wait_recv()

        @pl.when(core == 1)
        def _():
            across(c, 1, 4).start()

        across(c, 0, 0).wait_recv()
        across(c, 1, 0).wait_recv()

    def prepared(rows):
        qt = dot_nt(eye[...], rows)
        inverse = lax.rsqrt(jnp.mean(qt * qt, axis=0, keepdims=True) + EPSILON)
        gain = jnp.concatenate([gain_col[...]] * (qt.shape[1] // HEAD), axis=1)
        return qt, inverse, (qt * inverse * gain).astype(BF16)

    def query_backward(grad, qt, inverse):
        gain = jnp.concatenate([gain_col[...]] * (qt.shape[1] // HEAD), axis=1)
        both = grad * qt
        mean = jnp.mean(both * gain, axis=0, keepdims=True)
        scaled = inverse * SCALE
        out = grad * gain * scaled - qt * (inverse * inverse * scaled * mean)
        portion = both * scaled
        portion = sum(portion[:, at : at + HEAD] for at in range(0, qt.shape[1], HEAD))
        return out.T.astype(BF16), portion

    def prepare_prompt_keys(h):
        wide_k, inverse = normed_rows(kself[pl.ds(0, PROMPT), cols(h)])
        normed = (wide_k * inverse * kg[...]).astype(BF16)
        kn_p[h] = normed
        knt_p[h] = dot_nt(eye[...], normed).astype(BF16)

    half = PROMPT // 2

    def prompt_head(h):
        lo, hi = pl.ds(0, half), pl.ds(half, half)
        parts = []
        for pair in range(groups // 2):
            at = [cols(h, 2 * pair + i) for i in range(2)]
            parts.append((at, lo, lo, bias_lower, keep_lower))
            parts.append((at, hi, pl.ds(0, PROMPT), bias_upper, keep_upper))
        stacked = [jnp.concatenate([qv[r, a] for a in at], axis=0) for at, r, *_ in parts]
        ready = [prepared(x) for x in stacked]
        rows_o = [jnp.concatenate([ov[r, a] for a in at], axis=0) for at, r, *_ in parts]
        p_grad = [dot_nt(vself[p[2], cols(h)], x) for p, x in zip(parts, rows_o)]
        scores = [dot_nn(kn_p[h, p[2]], r[2]) + p[3][...] for p, r in zip(parts, ready)]
        probs = [softmax_columns([x], p[4])[0] for p, x in zip(parts, scores)]
        weights = [p.astype(BF16) for p in probs]
        s_grad = [score_gradient([p], [w], [g])[0] for p, w, g in zip(probs, weights, p_grad)]
        grad = [dot_nn(knt_p[h, :, p[2]], x) for p, x in zip(parts, s_grad)]
        dv = [dot_nn(w, x) for w, x in zip(weights, rows_o)]
        dk = [dot_nt(x, r[2]) for x, r in zip(s_grad, ready)]
        for total, terms in ((dv_acc, dv), (dk_acc, dk)):
            total[h, lo] += sum(terms[0::2]) + sum(t[:half] for t in terms[1::2])
            total[h, hi] += sum(t[half:] for t in terms[1::2])
        portions = []
        for p, x, g in zip(parts, ready, grad):
            out, portion = query_backward(g, x[0], x[1])
            portions.append(portion)
            for i, a in enumerate(p[0]):
                dqv[p[1], a] = out[i * half : (i + 1) * half]
        qg_acc[...] += sum(portions)

    def response_rows(s):
        return pl.ds(PROMPT + s * RESP, RESP)

    def prepare_responses(h):
        ready = []
        for s in range(2):
            rows = response_rows(s)
            stacked = jnp.concatenate([qv[rows, cols(h, g)] for g in range(groups)], axis=0)
            r_o[h, s] = jnp.concatenate([ov[rows, cols(h, g)] for g in range(groups)], axis=0)
            ready.append(prepared(stacked))
        for s, (qt, inverse, qnt) in enumerate(ready):
            r_qt[h, s] = qt
            r_qnt[h, s] = qnt
            r_inv[h, s] = jnp.broadcast_to(inverse, (8, inverse.shape[1]))
            wide_k, inverse = normed_rows(kself[response_rows(s), cols(h)])
            hat = wide_k * inverse
            r_khat[h, s, pl.ds(PROMPT, RESP)] = hat
            r_k[h, s, pl.ds(PROMPT, RESP)] = (hat * kg[...]).astype(BF16)

    span = 2 * HEAD
    firsts = range(0, groups * RESP, span)
    blocks = [(s, pl.ds(first, span), first) for s in range(2) for first in firsts]

    def response_keys(h):
        normed, bias, keep = [], [], []
        for s in range(2):
            wide_k, inverse = normed_rows(near[h][picks[s], pl.ds(0, PROMPT)])
            hat = wide_k * inverse
            r_khat[h, s, pl.ds(0, PROMPT)] = hat
            r_k[h, s, pl.ds(0, PROMPT)] = (hat * kg[...]).astype(BF16)
            normed.append(r_k[h, s])
            owner_length = near_k0[picks[s], pl.ds(PROMPT, 16)].astype(F32)[0:1]
            at = lax.broadcasted_iota(jnp.int32, (PROMPT, HEAD), 0).astype(F32)
            seen = jnp.where(at < owner_length, 0.0, MASKED)
            seen = jnp.concatenate([seen, bias_own[...]], axis=0)
            bias.append(jnp.concatenate([seen, seen], axis=1))
            place = lax.rem(lax.broadcasted_iota(jnp.int32, (1, span), 1), RESP)
            keep.append((place < rlen[s]).astype(F32))
        scores = [dot_nn(normed[s], r_qnt[h, s, :, b]) + bias[s] for s, b, _ in blocks]
        probs = [softmax_columns([x], keep[s])[0] for (s, _, _), x in zip(blocks, scores)]
        weights = [p.astype(BF16) for p in probs]
        terms = [dot_nn(w, r_o[h, s, b]) for (s, b, _), w in zip(blocks, weights)]
        for (s, b, _), p in zip(blocks, probs):
            r_p[h, s, :, b] = p
        half_way = len(terms) // 2
        totals = [sum(terms[:half_way]), sum(terms[half_way:])]
        give_back(heads + h, totals)
        for s in range(2):
            dv_out[response_rows(s), cols(h)] = totals[s][PROMPT:].astype(BF16)
            r_kt[h, s] = dot_nt(eye[...], normed[s]).astype(BF16)

    def response_values(h):
        rows_v = [
            jnp.concatenate([near[heads + h][picks[s]], vself[response_rows(s), cols(h)]], axis=0)
            for s in range(2)
        ]
        p_grad = [dot_nt(rows_v[s], r_o[h, s, b]) for s, b, _ in blocks]
        probs = [r_p[h, s, :, b] for s, b, _ in blocks]
        s_grad = [score_gradient([p], [p.astype(BF16)], [g])[0] for p, g in zip(probs, p_grad)]
        terms = [dot_nt(x, r_qnt[h, s, :, b]) for (s, b, _), x in zip(blocks, s_grad)]
        half_way = len(terms) // 2
        totals = [sum(terms[:half_way]), sum(terms[half_way:])]
        give_back(h, totals)
        grads = [dot_nn(r_kt[h, s], x) for (s, _, _), x in zip(blocks, s_grad)]
        portions = []
        for (s, b, first), grad in zip(blocks, grads):
            out, portion = query_backward(grad, r_qt[h, s, :, b], r_inv[h, s, 0:1, b])
            portions.append(portion)
            for i in range(span // RESP):
                dqv[response_rows(s), cols(h, first // RESP + i)] = out[i * RESP : (i + 1) * RESP]
        qg_acc[...] += sum(portions)
        portion = sum(totals[s] * r_khat[h, s] for s in range(2)) * SCALE
        kg_acc[...] += jnp.sum(portion.reshape(KEYS // 8, 8, HEAD), axis=0)
        for s in range(2):
            rows = response_rows(s)
            dk_out[rows, cols(h)] = key_backward(totals[s][PROMPT:], kself[rows, cols(h)])

    def key_backward(grad, rows):
        wide_k, inverse = normed_rows(rows)
        scaled = grad * kg[...]
        mean = jnp.mean(scaled * wide_k, axis=1, keepdims=True)
        factor = inverse * SCALE
        return (scaled * factor - wide_k * (inverse * inverse * factor * mean)).astype(BF16)

    def backward(kind, c, src, dst, device):
        return pltpu.make_async_remote_copy(
            src_ref=src,
            dst_ref=dst,
            send_sem=bwd_send.at[kind, c],
            recv_sem=bwd_recv.at[kind, c],
            device_id=device,
            device_id_type=MESH,
        )

    def back_across(c):
        return backward(0, c, back.at[c, pl.ds(0, 2)], back_sib.at[c], sibling)

    def back_far(c):
        return backward(1, c, back_o4.at[c], back_r4.at[c], down)

    def back_near(c):
        return backward(2, c, back_o2.at[c], back_r2.at[c], down)

    def give_back(c, terms):
        for i, distance in enumerate((1, 3, 2, 4)):
            chosen = [(pick == distance).astype(F32) for pick in picks]
            term = chosen[0] * terms[0][:PROMPT] + chosen[1] * terms[1][:PROMPT]
            back[c, i] = term.astype(BF16)
        back_across(c).start()

    upper = core.astype(F32)

    def give_back_far(c):
        back_across(c).wait_recv()
        total = back[c, 3].astype(F32) + upper * back_sib[c, 1].astype(F32)
        back_o4[c] = total.astype(BF16)
        back_far(c).start()

    def give_back_near(c):
        back_far(c).wait_recv()
        other = upper * back_sib[c, 0].astype(F32) + (1.0 - upper) * back_sib[c, 1].astype(F32)
        total = back[c, 2].astype(F32) + back_r4[c].astype(F32) + other
        back_o2[c] = total.astype(BF16)
        back_near(c).start()

    def taken_back(c):
        back_near(c).wait_recv()
        return back_r2[c].astype(F32) + (1.0 - upper) * back_sib[c, 0].astype(F32)

    def exchange(n, peer, place, source, buffer, send_sem, recv_sem):
        def copy(k):
            other, device = peer(k)
            return pltpu.make_async_remote_copy(
                src_ref=source,
                dst_ref=buffer.at[place],
                send_sem=send_sem.at[other],
                recv_sem=recv_sem.at[place],
                device_id=device,
                device_id_type=MESH,
            )

        def arriving(k):
            other, device = peer(k)
            return pltpu.make_async_remote_copy(
                src_ref=source,
                dst_ref=buffer.at[other],
                send_sem=send_sem.at[other],
                recv_sem=recv_sem.at[other],
                device_id=device,
                device_id_type=MESH,
            )

        def start():
            if n > 1:

                @pl.loop(1, n)
                def _(k):
                    copy(k).start()

        def collect():
            buffer[place] = source[...]
            if n > 1:

                @pl.loop(1, n)
                def _(k):
                    arriving(k).wait_recv()

            total = buffer[0]
            for i in range(1, n):
                total = total + buffer[i]
            return total

        def finish():
            if n > 1:

                @pl.loop(1, n)
                def _(k):
                    copy(k).wait_send()

        return start, collect, finish

    start_a, collect_a, finish_a = exchange(n_a, peer_a, place_a, part_a, buf_a, a_send, a_recv)
    start_b, collect_b, finish_b = exchange(16, peer_b, place_b, part_b, buf_b, b_send, b_recv)

    def prompt_key_portion():
        for h in range(heads):
            wide_k, inverse = normed_rows(kself[pl.ds(0, PROMPT), cols(h)])
            portion = dk_acc[h] * (wide_k * inverse) * SCALE
            kg_acc[...] += jnp.sum(portion.reshape(PROMPT // 8, 8, HEAD), axis=0)

    def sum_gains():
        part_a[...] = jnp.concatenate(
            [
                jnp.sum(qg_acc[...].T, axis=0, keepdims=True),
                jnp.sum(kg_acc[...], axis=0, keepdims=True),
                jnp.zeros((6, HEAD), F32),
            ],
            axis=0,
        )

    prompt = pl.ds(0, PROMPT)

    def finish_values(h):
        dv_out[prompt, cols(h)] = (dv_acc[h] + taken_back(heads + h)).astype(BF16)

    def finish_keys(h):
        dk_out[prompt, cols(h)] = key_backward(dk_acc[h] + taken_back(h), kself[prompt, cols(h)])

    for c in range(chunks):
        send_own(c)
    prepare()
    load_k.wait()
    load_v.wait()
    load_q[0].wait()
    load_o[0].wait()
    prepare_prompt_keys(0)
    prompt_head(0)
    load_q[1].wait()
    load_o[1].wait()
    prepare_responses(0)
    prepare_responses(1)
    pass_on(0)
    prepare_prompt_keys(1)
    prompt_head(1)
    pass_on(1)
    prompt_key_portion()
    pass_on(2)
    pass_on(3)
    arrive(0)
    response_keys(0)
    arrive(1)
    response_keys(1)
    give_back_far(2)
    arrive(2)
    response_values(0)
    give_back_far(3)
    arrive(3)
    response_values(1)
    sum_gains()
    start_a()
    give_back_far(0)
    give_back_far(1)
    give_back_near(2)
    give_back_near(3)
    give_back_near(0)
    part_b[...] = collect_a()
    start_b()
    give_back_near(1)
    for h in range(heads):
        finish_values(h)
    for h in range(heads):
        finish_keys(h)
    gains_out[...] = collect_b()

    finish_a()
    finish_b()
    for c in range(chunks):
        hop(c).wait_send()
        relay(c).wait_send()
        across(c, 0, 0).wait_send()
        across(c, 1, 0).wait_send()
        back_across(c).wait_send()
        back_far(c).wait_send()
        back_near(c).wait_send()


def hand_out(q, k, v, gains, q_out, k_out, v_out, qg_out, kg_out, sems):
    copies = [
        pltpu.make_async_copy(src, dst, sems.at[i])
        for i, (src, dst) in enumerate(
            [
                (q, q_out),
                (k, k_out),
                (v, v_out),
                (gains.at[0:1], qg_out),
                (gains.at[1:2], kg_out),
            ]
        )
    ]
    for copy in copies:
        copy.start()
    for copy in copies:
        copy.wait()


def on_device(
    n_dp, n_tensor, queries, keys, values, output_gradient, q_gain, k_gain, prompt_len, resp_len, resp_owner
):
    heads = keys.shape[1] // HEAD
    groups = queries.shape[1] // keys.shape[1]
    rows = queries.shape[0]
    chunks = 2 * heads
    n_a = n_dp // 16 * n_tensor
    vmem = pl.BlockSpec(memory_space=pltpu.VMEM)
    smem = pl.BlockSpec(memory_space=pltpu.SMEM)
    hbm = pl.BlockSpec(memory_space=pltpu.HBM)
    asked = groups * RESP
    scratch = [
        pltpu.VMEM(queries.shape, BF16),
        pltpu.VMEM(queries.shape, BF16),
        pltpu.VMEM(keys.shape, BF16),
        pltpu.VMEM(keys.shape, BF16),
        pltpu.VMEM((5, PROMPT + 16, HEAD), BF16),
        pltpu.VMEM((5, PROMPT, HEAD), BF16),
        pltpu.VMEM((5, PROMPT, HEAD), BF16),
        pltpu.VMEM((5, PROMPT, HEAD), BF16),
        pltpu.VMEM((HEAD, HEAD), BF16),
        pltpu.VMEM((HEAD, HEAD), F32),
        pltpu.VMEM((PROMPT // 2, PROMPT), F32),
        pltpu.VMEM((PROMPT, PROMPT), F32),
        pltpu.VMEM((RESP, HEAD), F32),
        pltpu.VMEM((heads, PROMPT, HEAD), BF16),
        pltpu.VMEM((heads, HEAD, PROMPT), BF16),
        pltpu.VMEM((heads, PROMPT, HEAD), F32),
        pltpu.VMEM((heads, PROMPT, HEAD), F32),
        pltpu.VMEM((HEAD, HEAD), F32),
        pltpu.VMEM((8, HEAD), F32),
        pltpu.VMEM((heads, 2, asked, HEAD), BF16),
        pltpu.VMEM((heads, 2, HEAD, asked), F32),
        pltpu.VMEM((heads, 2, HEAD, asked), BF16),
        pltpu.VMEM((heads, 2, 8, asked), F32),
        pltpu.VMEM((heads, 2, KEYS, HEAD), BF16),
        pltpu.VMEM((heads, 2, HEAD, KEYS), BF16),
        pltpu.VMEM((heads, 2, KEYS, HEAD), F32),
        pltpu.VMEM((heads, 2, KEYS, asked), F32),
        pltpu.VMEM((chunks, 4, PROMPT, HEAD), BF16),
        pltpu.VMEM((chunks, 2, PROMPT, HEAD), BF16),
        pltpu.VMEM((chunks, PROMPT, HEAD), BF16),
        pltpu.VMEM((chunks, PROMPT, HEAD), BF16),
        pltpu.VMEM((chunks, PROMPT, HEAD), BF16),
        pltpu.VMEM((chunks, PROMPT, HEAD), BF16),
        pltpu.VMEM((8, HEAD), F32),
        pltpu.VMEM((8, HEAD), F32),
        pltpu.VMEM((n_a, 8, HEAD), F32),
        pltpu.VMEM((16, 8, HEAD), F32),
        pltpu.SemaphoreType.DMA((chunks + 2 + 2 * heads,)),
        pltpu.SemaphoreType.DMA((4, chunks)),
        pltpu.SemaphoreType.DMA((4, chunks)),
        pltpu.SemaphoreType.DMA((3, chunks)),
        pltpu.SemaphoreType.DMA((3, chunks)),
        pltpu.SemaphoreType.DMA((n_a,)),
        pltpu.SemaphoreType.DMA((n_a,)),
        pltpu.SemaphoreType.DMA((16,)),
        pltpu.SemaphoreType.DMA((16,)),
    ]
    results = pl.pallas_call(
        functools.partial(kernel, heads, groups, n_dp, n_tensor),
        out_shape=(
            pltpu.VMEM(queries.shape, BF16),
            pltpu.VMEM(keys.shape, BF16),
            pltpu.VMEM(keys.shape, BF16),
            pltpu.VMEM((8, HEAD), F32),
        ),
        in_specs=[smem, smem, smem, vmem, vmem, hbm, hbm, hbm, hbm],
        out_specs=(vmem, vmem, vmem, vmem),
        scratch_shapes=scratch,
        compiler_params=pltpu.CompilerParams(
            collective_id=0, has_side_effects=True, vmem_limit_bytes=56 * 2**20
        ),
        name="attention",
    )(
        prompt_len,
        resp_len,
        resp_owner,
        q_gain.reshape(1, HEAD),
        k_gain.reshape(1, HEAD),
        *[
            pltpu.with_memory_space_constraint(a, pltpu.HBM)
            for a in (queries, keys, values, output_gradient)
        ],
    )
    q_grad, k_grad, v_grad, q_gain_grad, k_gain_grad = pl.pallas_call(
        hand_out,
        out_shape=(
            jax.ShapeDtypeStruct(queries.shape, BF16),
            jax.ShapeDtypeStruct(keys.shape, BF16),
            jax.ShapeDtypeStruct(keys.shape, BF16),
            jax.ShapeDtypeStruct((1, HEAD), F32),
            jax.ShapeDtypeStruct((1, HEAD), F32),
        ),
        in_specs=[vmem] * 4,
        out_specs=(hbm,) * 5,
        scratch_shapes=[pltpu.SemaphoreType.DMA((5,))],
        name="hand_out",
    )(*results)
    return q_grad, k_grad, v_grad, q_gain_grad.reshape(HEAD), k_gain_grad.reshape(HEAD)


def solution(mesh):
    rows, whole = P("dp", "tensor"), P()
    return jax.shard_map(
        functools.partial(on_device, mesh.shape["dp"], mesh.shape["tensor"]),
        mesh=mesh,
        in_specs=(rows, rows, rows, rows, whole, whole, P("dp"), P("dp"), P("dp")),
        out_specs=(rows, rows, rows, whole, whole),
        check_vma=False,
    )
```

```python
import functools

import jax
import jax.numpy as jnp
from jax import lax
from jax.experimental import pallas as pl
from jax.experimental.pallas import tpu as pltpu
from jax.sharding import PartitionSpec as P

PROMPT = 256
RESP = 64
HEAD = 128
KEYS = PROMPT + RESP
EPSILON = 1e-06
SCALE = HEAD ** (-0.5)
LOG2E = 1.4426950408889634
SHARP = SCALE * LOG2E
MASKED = -1e30
MESH = pl.DeviceIdType.MESH
F32 = jnp.float32
BF16 = jnp.bfloat16
NT = (((1,), (1,)), ((), ()))


def dot_nn(a, b):
    return jnp.dot(a, b, preferred_element_type=F32)


def dot_nt(a, b):
    return lax.dot_general(a, b, NT, preferred_element_type=F32)


def normed_rows(rows):
    wide = rows.astype(F32)
    inverse = lax.rsqrt(jnp.mean(wide * wide, axis=1, keepdims=True) + EPSILON)
    return wide, inverse


def softmax_columns(blocks, keep):
    top = functools.reduce(jnp.maximum, [jnp.max(b, axis=0, keepdims=True) for b in blocks])
    shift = top * SHARP
    raised = [jnp.exp2(b * SHARP - shift) for b in blocks]
    total = functools.reduce(jnp.add, [jnp.sum(b, axis=0, keepdims=True) for b in raised])
    factor = keep / total
    return [b * factor for b in raised]


def score_gradient(probs, weights, p_grads):
    inner = functools.reduce(
        jnp.add,
        [
            jnp.sum(w.astype(F32) * g, axis=0, keepdims=True)
            for w, g in zip(weights, p_grads, strict=True)
        ],
    )
    return [(p * (g - inner)).astype(BF16) for p, g in zip(probs, p_grads, strict=True)]


def kernel(
    heads,
    groups,
    n_dp,
    n_tensor,
    plen,
    rlen,
    rown,
    qg,
    kg,
    q_hbm,
    k_hbm,
    v_hbm,
    o_hbm,
    dqv,
    dk_out,
    dv_out,
    gains_out,
    qv,
    ov,
    length_at,
    kself,
    vself,
    near_k0,
    near_k1,
    near_v0,
    near_v1,
    eye,
    gain_col,
    bias_lower,
    bias_upper,
    bias_own,
    kn_p,
    knt_p,
    dk_acc,
    dv_acc,
    qg_acc,
    kg_acc,
    r_o,
    r_qt,
    r_qnt,
    r_inv,
    r_k,
    r_kt,
    r_khat,
    r_p,
    back,
    back_sib,
    back_r4,
    back_r2,
    back_o4,
    back_o2,
    part_a,
    part_b,
    buf_a,
    buf_b,
    load_sem,
    fwd_send,
    fwd_recv,
    bwd_send,
    bwd_recv,
    a_send,
    a_recv,
    b_send,
    b_recv,
):
    dp = lax.axis_index("dp")
    tensor = lax.axis_index("tensor")
    core = lax.rem(dp, 2)
    up = (lax.rem(dp + 2, n_dp), tensor)
    down = (lax.rem(dp + n_dp - 2, n_dp), tensor)
    far_up = (lax.rem(dp + 4, n_dp), tensor)
    far_down = (lax.rem(dp + n_dp - 4, n_dp), tensor)
    sibling = (dp + 1 - 2 * core, tensor)
    near = (near_k0, near_k1, near_v0, near_v1)
    chunks = 2 * heads

    columns = n_dp // 16
    n_a = columns * n_tensor
    place_a = lax.div(dp, 16) * n_tensor + tensor
    place_b = lax.rem(dp, 16)

    def within(at, size):
        return jnp.where(at < size, at, at - size)

    column = lax.div(dp, 16)
    peers_a = []
    for i in range(columns):
        for j in range(n_tensor):
            if i or j:
                at, side = within(column + i, columns), within(tensor + j, n_tensor)
                peers_a.append((at * n_tensor + side, (at * 16 + place_b, side)))
    peers_b = []
    for k in range(1, 16):
        at = within(place_b + k, 16)
        peers_b.append((at, (dp - place_b + at, tensor)))

    def cols(h, g=None):
        if g is None:
            return pl.ds(h * HEAD, HEAD)
        return pl.ds(pl.multiple_of((h * groups + g) * HEAD, HEAD), HEAD)

    loads = []

    def load(src, dst):
        copy = pltpu.make_async_copy(src, dst, load_sem.at[len(loads)])
        copy.start()
        loads.append(copy)
        return copy

    staged = []
    for c in range(chunks):
        h = c % heads
        source = (k_hbm if c < heads else v_hbm).at[pl.ds(0, PROMPT), cols(h)]
        staged.append(load(source, near[c].at[0, pl.ds(0, PROMPT)]))
    load_length = load(plen, length_at)
    load_k = load(k_hbm, kself)
    wide = groups * HEAD
    load_q, load_o = [], []
    for h in range(heads):
        load_q.append(load(q_hbm.at[:, pl.ds(h * wide, wide)], qv.at[:, pl.ds(h * wide, wide)]))
        load_o.append(load(o_hbm.at[:, pl.ds(h * wide, wide)], ov.at[:, pl.ds(h * wide, wide)]))
        if h == 0:
            load_v = load(v_hbm, vself)

    barrier = pltpu.get_barrier_semaphore()
    greeted = [up, down, far_up, far_down] + [device for _, device in peers_b + peers_a]
    for device in greeted:
        pl.semaphore_signal(barrier, inc=1, device_id=device, device_id_type=MESH)

    load_length.wait()
    length = length_at[0]
    query_at = lax.rem(lax.broadcasted_iota(jnp.int32, (1, PROMPT), 1), PROMPT // 2)
    keep_lower = (query_at < length).astype(F32)
    keep_upper = (query_at + PROMPT // 2 < length).astype(F32)
    near_k0[0, pl.ds(PROMPT, 16)] = jnp.full((16, HEAD), length.astype(F32)).astype(BF16)

    def prepare():
        row_at = lax.broadcasted_iota(jnp.int32, (HEAD, HEAD), 0)
        col_at = lax.broadcasted_iota(jnp.int32, (HEAD, HEAD), 1)
        eye[...] = jnp.where(row_at == col_at, 1.0, 0.0).astype(BF16)
        gain_col[...] = jnp.broadcast_to(qg[...], (HEAD, HEAD)).T
        for lower, bias in ((True, bias_lower), (False, bias_upper)):
            key_at = lax.broadcasted_iota(jnp.int32, bias.shape, 0)
            query_at = lax.rem(lax.broadcasted_iota(jnp.int32, bias.shape, 1), PROMPT // 2)
            query_at = query_at if lower else query_at + PROMPT // 2
            bias[...] = jnp.where((key_at <= query_at) & (key_at < length), 0.0, MASKED)
        own_key = lax.broadcasted_iota(jnp.int32, (RESP, HEAD), 0)
        own_query = lax.rem(lax.broadcasted_iota(jnp.int32, (RESP, HEAD), 1), RESP)
        bias_own[...] = jnp.where(own_key <= own_query, 0.0, MASKED)
        qg_acc[...] = jnp.zeros_like(qg_acc)
        kg_acc[...] = jnp.zeros_like(kg_acc)
        dk_acc[...] = jnp.zeros_like(dk_acc)
        dv_acc[...] = jnp.zeros_like(dv_acc)

    picks = [jnp.clip(lax.rem(dp + n_dp - rown[s], n_dp), 1, 4) for s in range(2)]

    for copy in staged:
        copy.wait()
    pl.semaphore_wait(barrier, len(greeted))

    def slot(c, d):
        return near[c].at[d]

    def forward(kind, c, src, dst, device):
        return pltpu.make_async_remote_copy(
            src_ref=slot(c, src),
            dst_ref=slot(c, dst),
            send_sem=fwd_send.at[kind, c],
            recv_sem=fwd_recv.at[kind, c],
            device_id=device,
            device_id_type=MESH,
        )

    def hop(c):
        return forward(0, c, 0, 2, up)

    def relay(c):
        return forward(1, c, 2, 4, up)

    def across(c, far, src):
        return forward(2 + far, c, src, 1 + 2 * far, sibling)

    def send_own(c):
        hop(c).start()

        @pl.when(core == 0)
        def _():
            across(c, 0, 0).start()

    def pass_on(c):
        hop(c).wait_recv()
        relay(c).start()

        @pl.when(core == 0)
        def _():
            across(c, 1, 2).start()

        @pl.when(core == 1)
        def _():
            across(c, 0, 2).start()

    def arrive(c):
        relay(c).wait_recv()

        @pl.when(core == 1)
        def _():
            across(c, 1, 4).start()

        across(c, 0, 0).wait_recv()
        across(c, 1, 0).wait_recv()

    def prepared(rows):
        qt = dot_nt(eye[...], rows)
        inverse = lax.rsqrt(jnp.mean(qt * qt, axis=0, keepdims=True) + EPSILON)
        gain = jnp.concatenate([gain_col[...]] * (qt.shape[1] // HEAD), axis=1)
        return qt, inverse, (qt * inverse * gain).astype(BF16)

    def query_backward(grad, qt, inverse):
        gain = jnp.concatenate([gain_col[...]] * (qt.shape[1] // HEAD), axis=1)
        both = grad * qt
        mean = jnp.mean(both * gain, axis=0, keepdims=True)
        scaled = inverse * SCALE
        out = grad * gain * scaled - qt * (inverse * inverse * scaled * mean)
        portion = both * scaled
        portion = sum(portion[:, at : at + HEAD] for at in range(0, qt.shape[1], HEAD))
        return out.T.astype(BF16), portion

    def prepare_prompt_keys(h):
        wide_k, inverse = normed_rows(kself[pl.ds(0, PROMPT), cols(h)])
        normed = (wide_k * inverse * kg[...]).astype(BF16)
        kn_p[h] = normed
        knt_p[h] = dot_nt(eye[...], normed).astype(BF16)

    half = PROMPT // 2

    def prompt_head(h):
        lo, hi = pl.ds(0, half), pl.ds(half, half)
        parts = []
        for pair in range(groups // 2):
            at = [cols(h, 2 * pair + i) for i in range(2)]
            parts.append((at, lo, lo, bias_lower, keep_lower))
            parts.append((at, hi, pl.ds(0, PROMPT), bias_upper, keep_upper))
        stacked = [jnp.concatenate([qv[r, a] for a in at], axis=0) for at, r, *_ in parts]
        ready = [prepared(x) for x in stacked]
        rows_o = [jnp.concatenate([ov[r, a] for a in at], axis=0) for at, r, *_ in parts]
        p_grad = [dot_nt(vself[p[2], cols(h)], x) for p, x in zip(parts, rows_o)]
        scores = [dot_nn(kn_p[h, p[2]], r[2]) + p[3][...] for p, r in zip(parts, ready)]
        probs = [softmax_columns([x], p[4])[0] for p, x in zip(parts, scores)]
        weights = [p.astype(BF16) for p in probs]
        s_grad = [score_gradient([p], [w], [g])[0] for p, w, g in zip(probs, weights, p_grad)]
        grad = [dot_nn(knt_p[h, :, p[2]], x) for p, x in zip(parts, s_grad)]
        dv = [dot_nn(w, x) for w, x in zip(weights, rows_o)]
        dk = [dot_nt(x, r[2]) for x, r in zip(s_grad, ready)]
        for total, terms in ((dv_acc, dv), (dk_acc, dk)):
            total[h, lo] += sum(terms[0::2]) + sum(t[:half] for t in terms[1::2])
            total[h, hi] += sum(t[half:] for t in terms[1::2])
        portions = []
        for p, x, g in zip(parts, ready, grad):
            out, portion = query_backward(g, x[0], x[1])
            portions.append(portion)
            for i, a in enumerate(p[0]):
                dqv[p[1], a] = out[i * half : (i + 1) * half]
        qg_acc[...] += sum(portions)

    def response_rows(s):
        return pl.ds(PROMPT + s * RESP, RESP)

    def prepare_responses(h):
        ready = []
        for s in range(2):
            rows = response_rows(s)
            stacked = jnp.concatenate([qv[rows, cols(h, g)] for g in range(groups)], axis=0)
            r_o[h, s] = jnp.concatenate([ov[rows, cols(h, g)] for g in range(groups)], axis=0)
            ready.append(prepared(stacked))
        for s, (qt, inverse, qnt) in enumerate(ready):
            r_qt[h, s] = qt
            r_qnt[h, s] = qnt
            r_inv[h, s] = jnp.broadcast_to(inverse, (8, inverse.shape[1]))
            wide_k, inverse = normed_rows(kself[response_rows(s), cols(h)])
            hat = wide_k * inverse
            r_khat[h, s, pl.ds(PROMPT, RESP)] = hat
            r_k[h, s, pl.ds(PROMPT, RESP)] = (hat * kg[...]).astype(BF16)

    span = 2 * HEAD
    firsts = range(0, groups * RESP, span)
    blocks = [(s, pl.ds(first, span), first) for s in range(2) for first in firsts]

    def response_keys(h):
        normed, bias, keep = [], [], []
        for s in range(2):
            wide_k, inverse = normed_rows(near[h][picks[s], pl.ds(0, PROMPT)])
            hat = wide_k * inverse
            r_khat[h, s, pl.ds(0, PROMPT)] = hat
            r_k[h, s, pl.ds(0, PROMPT)] = (hat * kg[...]).astype(BF16)
            normed.append(r_k[h, s])
            owner_length = near_k0[picks[s], pl.ds(PROMPT, 16)].astype(F32)[0:1]
            at = lax.broadcasted_iota(jnp.int32, (PROMPT, HEAD), 0).astype(F32)
            seen = jnp.where(at < owner_length, 0.0, MASKED)
            seen = jnp.concatenate([seen, bias_own[...]], axis=0)
            bias.append(jnp.concatenate([seen, seen], axis=1))
            place = lax.rem(lax.broadcasted_iota(jnp.int32, (1, span), 1), RESP)
            keep.append((place < rlen[s]).astype(F32))
        scores = [dot_nn(normed[s], r_qnt[h, s, :, b]) + bias[s] for s, b, _ in blocks]
        probs = [softmax_columns([x], keep[s])[0] for (s, _, _), x in zip(blocks, scores)]
        weights = [p.astype(BF16) for p in probs]
        terms = [dot_nn(w, r_o[h, s, b]) for (s, b, _), w in zip(blocks, weights)]
        for (s, b, _), p in zip(blocks, probs):
            r_p[h, s, :, b] = p
        half_way = len(terms) // 2
        totals = [sum(terms[:half_way]), sum(terms[half_way:])]
        give_back(heads + h, totals)
        for s in range(2):
            dv_out[response_rows(s), cols(h)] = totals[s][PROMPT:].astype(BF16)
            r_kt[h, s] = dot_nt(eye[...], normed[s]).astype(BF16)

    def response_values(h):
        rows_v = [
            jnp.concatenate([near[heads + h][picks[s]], vself[response_rows(s), cols(h)]], axis=0)
            for s in range(2)
        ]
        p_grad = [dot_nt(rows_v[s], r_o[h, s, b]) for s, b, _ in blocks]
        probs = [r_p[h, s, :, b] for s, b, _ in blocks]
        s_grad = [score_gradient([p], [p.astype(BF16)], [g])[0] for p, g in zip(probs, p_grad)]
        terms = [dot_nt(x, r_qnt[h, s, :, b]) for (s, b, _), x in zip(blocks, s_grad)]
        half_way = len(terms) // 2
        totals = [sum(terms[:half_way]), sum(terms[half_way:])]
        give_back(h, totals)
        grads = [dot_nn(r_kt[h, s], x) for (s, _, _), x in zip(blocks, s_grad)]
        portions = []
        for (s, b, first), grad in zip(blocks, grads):
            out, portion = query_backward(grad, r_qt[h, s, :, b], r_inv[h, s, 0:1, b])
            portions.append(portion)
            for i in range(span // RESP):
                dqv[response_rows(s), cols(h, first // RESP + i)] = out[i * RESP : (i + 1) * RESP]
        qg_acc[...] += sum(portions)
        portion = sum(totals[s] * r_khat[h, s] for s in range(2)) * SCALE
        kg_acc[...] += jnp.sum(portion.reshape(KEYS // 8, 8, HEAD), axis=0)
        for s in range(2):
            rows = response_rows(s)
            dk_out[rows, cols(h)] = key_backward(totals[s][PROMPT:], kself[rows, cols(h)])

    def key_backward(grad, rows):
        wide_k, inverse = normed_rows(rows)
        scaled = grad * kg[...]
        mean = jnp.mean(scaled * wide_k, axis=1, keepdims=True)
        factor = inverse * SCALE
        return (scaled * factor - wide_k * (inverse * inverse * factor * mean)).astype(BF16)

    def backward(kind, c, src, dst, device):
        return pltpu.make_async_remote_copy(
            src_ref=src,
            dst_ref=dst,
            send_sem=bwd_send.at[kind, c],
            recv_sem=bwd_recv.at[kind, c],
            device_id=device,
            device_id_type=MESH,
        )

    def back_across(c):
        return backward(0, c, back.at[c, pl.ds(0, 2)], back_sib.at[c], sibling)

    def back_far(c):
        return backward(1, c, back_o4.at[c], back_r4.at[c], down)

    def back_direct(c):
        return backward(1, c, back_o4.at[c], back_r4.at[c], far_down)

    def back_near(c):
        return backward(2, c, back_o2.at[c], back_r2.at[c], down)

    def give_back(c, terms):
        for i, distance in enumerate((1, 3, 2, 4)):
            chosen = [(pick == distance).astype(F32) for pick in picks]
            term = chosen[0] * terms[0][:PROMPT] + chosen[1] * terms[1][:PROMPT]
            back[c, i] = term.astype(BF16)
        back_across(c).start()

    upper = core.astype(F32)

    def give_back_far(c):
        back_across(c).wait_recv()
        total = back[c, 3].astype(F32) + upper * back_sib[c, 1].astype(F32)
        back_o4[c] = total.astype(BF16)
        back_far(c).start()

    def give_back_near(c):
        back_far(c).wait_recv()
        other = upper * back_sib[c, 0].astype(F32) + (1.0 - upper) * back_sib[c, 1].astype(F32)
        total = back[c, 2].astype(F32) + back_r4[c].astype(F32) + other
        back_o2[c] = total.astype(BF16)
        back_near(c).start()

    def give_back_direct(c):
        back_across(c).wait_recv()
        total = back[c, 3].astype(F32) + upper * back_sib[c, 1].astype(F32)
        back_o4[c] = total.astype(BF16)
        back_direct(c).start()
        other = upper * back_sib[c, 0].astype(F32) + (1.0 - upper) * back_sib[c, 1].astype(F32)
        back_o2[c] = (back[c, 2].astype(F32) + other).astype(BF16)
        back_near(c).start()

    def taken_back(c, direct=False):
        back_near(c).wait_recv()
        total = back_r2[c].astype(F32) + (1.0 - upper) * back_sib[c, 0].astype(F32)
        if direct:
            back_direct(c).wait_recv()
            total = total + back_r4[c].astype(F32)
        return total

    def exchange(peers, place, source, buffer, send_sem, recv_sem):
        def copy(other, device, slot):
            return pltpu.make_async_remote_copy(
                src_ref=source,
                dst_ref=buffer.at[slot],
                send_sem=send_sem.at[other],
                recv_sem=recv_sem.at[slot],
                device_id=device,
                device_id_type=MESH,
            )

        def start():
            for other, device in peers:
                copy(other, device, place).start()
            buffer[place] = source[...]

        def collect():
            for other, device in peers:
                copy(other, device, other).wait_recv()
            total = buffer[0]
            for i in range(1, len(peers) + 1):
                total = total + buffer[i]
            return total

        def finish():
            for other, device in peers:
                copy(other, device, place).wait_send()

        return start, collect, finish

    start_a, collect_a, finish_a = exchange(peers_b, place_b, part_b, buf_b, b_send, b_recv)
    start_b, collect_b, finish_b = exchange(peers_a, place_a, part_a, buf_a, a_send, a_recv)

    def prompt_key_portion():
        for h in range(heads):
            wide_k, inverse = normed_rows(kself[pl.ds(0, PROMPT), cols(h)])
            portion = dk_acc[h] * (wide_k * inverse) * SCALE
            kg_acc[...] += jnp.sum(portion.reshape(PROMPT // 8, 8, HEAD), axis=0)

    def sum_gains():
        part_b[...] = jnp.concatenate(
            [
                jnp.sum(qg_acc[...].T, axis=0, keepdims=True),
                jnp.sum(kg_acc[...], axis=0, keepdims=True),
                jnp.zeros((6, HEAD), F32),
            ],
            axis=0,
        )

    prompt = pl.ds(0, PROMPT)

    def finish_values(h):
        dv_out[prompt, cols(h)] = (dv_acc[h] + taken_back(heads + h)).astype(BF16)

    def finish_keys(h):
        total = dk_acc[h] + taken_back(h)
        dk_out[prompt, cols(h)] = key_backward(total, kself[prompt, cols(h)])

    for c in range(chunks):
        send_own(c)
    prepare()
    load_k.wait()
    load_v.wait()
    load_q[0].wait()
    load_o[0].wait()
    prepare_prompt_keys(0)
    prompt_head(0)
    load_q[1].wait()
    load_o[1].wait()
    prepare_responses(0)
    prepare_responses(1)
    pass_on(0)
    prepare_prompt_keys(1)
    prompt_head(1)
    pass_on(1)
    prompt_key_portion()
    pass_on(2)
    pass_on(3)
    arrive(0)
    response_keys(0)
    arrive(1)
    response_keys(1)
    give_back_far(2)
    arrive(2)
    response_values(0)
    give_back_far(3)
    arrive(3)
    response_values(1)
    sum_gains()
    start_a()
    give_back_far(0)
    give_back_far(1)
    give_back_near(2)
    give_back_near(3)
    part_a[...] = collect_a()
    start_b()
    give_back_near(0)
    give_back_near(1)
    for h in range(heads):
        finish_values(h)
    for h in range(heads):
        finish_keys(h)
    gains_out[...] = collect_b()

    finish_a()
    finish_b()
    for c in range(chunks):
        hop(c).wait_send()
        relay(c).wait_send()
        across(c, 0, 0).wait_send()
        across(c, 1, 0).wait_send()
        back_across(c).wait_send()
        back_far(c).wait_send()
        back_near(c).wait_send()


def hand_out(q, k, v, gains, q_out, k_out, v_out, qg_out, kg_out, sems):
    copies = [
        pltpu.make_async_copy(src, dst, sems.at[i])
        for i, (src, dst) in enumerate(
            [
                (q, q_out),
                (k, k_out),
                (v, v_out),
                (gains.at[0:1], qg_out),
                (gains.at[1:2], kg_out),
            ]
        )
    ]
    for copy in copies:
        copy.start()
    for copy in copies:
        copy.wait()


def on_device(
    n_dp, n_tensor, queries, keys, values, output_gradient, q_gain, k_gain, prompt_len, resp_len, resp_owner
):
    heads = keys.shape[1] // HEAD
    groups = queries.shape[1] // keys.shape[1]
    rows = queries.shape[0]
    chunks = 2 * heads
    n_a = n_dp // 16 * n_tensor
    vmem = pl.BlockSpec(memory_space=pltpu.VMEM)
    smem = pl.BlockSpec(memory_space=pltpu.SMEM)
    hbm = pl.BlockSpec(memory_space=pltpu.HBM)
    asked = groups * RESP
    scratch = [
        pltpu.VMEM(queries.shape, BF16),
        pltpu.VMEM(queries.shape, BF16),
        pltpu.SMEM((1,), jnp.int32),
        pltpu.VMEM(keys.shape, BF16),
        pltpu.VMEM(keys.shape, BF16),
        pltpu.VMEM((5, PROMPT + 16, HEAD), BF16),
        pltpu.VMEM((5, PROMPT, HEAD), BF16),
        pltpu.VMEM((5, PROMPT, HEAD), BF16),
        pltpu.VMEM((5, PROMPT, HEAD), BF16),
        pltpu.VMEM((HEAD, HEAD), BF16),
        pltpu.VMEM((HEAD, HEAD), F32),
        pltpu.VMEM((PROMPT // 2, PROMPT), F32),
        pltpu.VMEM((PROMPT, PROMPT), F32),
        pltpu.VMEM((RESP, HEAD), F32),
        pltpu.VMEM((heads, PROMPT, HEAD), BF16),
        pltpu.VMEM((heads, HEAD, PROMPT), BF16),
        pltpu.VMEM((heads, PROMPT, HEAD), F32),
        pltpu.VMEM((heads, PROMPT, HEAD), F32),
        pltpu.VMEM((HEAD, HEAD), F32),
        pltpu.VMEM((8, HEAD), F32),
        pltpu.VMEM((heads, 2, asked, HEAD), BF16),
        pltpu.VMEM((heads, 2, HEAD, asked), F32),
        pltpu.VMEM((heads, 2, HEAD, asked), BF16),
        pltpu.VMEM((heads, 2, 8, asked), F32),
        pltpu.VMEM((heads, 2, KEYS, HEAD), BF16),
        pltpu.VMEM((heads, 2, HEAD, KEYS), BF16),
        pltpu.VMEM((heads, 2, KEYS, HEAD), F32),
        pltpu.VMEM((heads, 2, KEYS, asked), F32),
        pltpu.VMEM((chunks, 4, PROMPT, HEAD), BF16),
        pltpu.VMEM((chunks, 2, PROMPT, HEAD), BF16),
        pltpu.VMEM((chunks, PROMPT, HEAD), BF16),
        pltpu.VMEM((chunks, PROMPT, HEAD), BF16),
        pltpu.VMEM((chunks, PROMPT, HEAD), BF16),
        pltpu.VMEM((chunks, PROMPT, HEAD), BF16),
        pltpu.VMEM((8, HEAD), F32),
        pltpu.VMEM((8, HEAD), F32),
        pltpu.VMEM((n_a, 8, HEAD), F32),
        pltpu.VMEM((16, 8, HEAD), F32),
        pltpu.SemaphoreType.DMA((chunks + 3 + 2 * heads,)),
        pltpu.SemaphoreType.DMA((4, chunks)),
        pltpu.SemaphoreType.DMA((4, chunks)),
        pltpu.SemaphoreType.DMA((3, chunks)),
        pltpu.SemaphoreType.DMA((3, chunks)),
        pltpu.SemaphoreType.DMA((n_a,)),
        pltpu.SemaphoreType.DMA((n_a,)),
        pltpu.SemaphoreType.DMA((16,)),
        pltpu.SemaphoreType.DMA((16,)),
    ]
    results = pl.pallas_call(
        functools.partial(kernel, heads, groups, n_dp, n_tensor),
        out_shape=(
            pltpu.VMEM(queries.shape, BF16),
            pltpu.VMEM(keys.shape, BF16),
            pltpu.VMEM(keys.shape, BF16),
            pltpu.VMEM((8, HEAD), F32),
        ),
        in_specs=[hbm, smem, smem, vmem, vmem, hbm, hbm, hbm, hbm],
        out_specs=(vmem, vmem, vmem, vmem),
        scratch_shapes=scratch,
        compiler_params=pltpu.CompilerParams(
            collective_id=0, has_side_effects=True, vmem_limit_bytes=56 * 2**20
        ),
        name="attention",
    )(
        prompt_len,
        resp_len,
        resp_owner,
        q_gain.reshape(1, HEAD),
        k_gain.reshape(1, HEAD),
        *[
            pltpu.with_memory_space_constraint(a, pltpu.HBM)
            for a in (queries, keys, values, output_gradient)
        ],
    )
    q_grad, k_grad, v_grad, q_gain_grad, k_gain_grad = pl.pallas_call(
        hand_out,
        out_shape=(
            jax.ShapeDtypeStruct(queries.shape, BF16),
            jax.ShapeDtypeStruct(keys.shape, BF16),
            jax.ShapeDtypeStruct(keys.shape, BF16),
            jax.ShapeDtypeStruct((1, HEAD), F32),
            jax.ShapeDtypeStruct((1, HEAD), F32),
        ),
        in_specs=[vmem] * 4,
        out_specs=(hbm,) * 5,
        scratch_shapes=[pltpu.SemaphoreType.DMA((5,))],
        compiler_params=pltpu.CompilerParams(vmem_limit_bytes=16 * 2**20),
        name="hand_out",
    )(*[pltpu.with_memory_space_constraint(x, pltpu.VMEM) for x in results])
    return q_grad, k_grad, v_grad, q_gain_grad.reshape(HEAD), k_gain_grad.reshape(HEAD)


def solution(mesh):
    rows, whole = P("dp", "tensor"), P()
    return jax.shard_map(
        functools.partial(on_device, mesh.shape["dp"], mesh.shape["tensor"]),
        mesh=mesh,
        in_specs=(rows, rows, rows, rows, whole, whole, P("dp"), P("dp"), P("dp")),
        out_specs=(rows, rows, rows, whole, whole),
        check_vma=False,
    )
```

```python
import functools

import jax
import jax.numpy as jnp
from jax import lax
from jax.experimental import pallas as pl
from jax.experimental.pallas import tpu as pltpu
from jax.sharding import PartitionSpec as P

PROMPT = 256
RESP = 64
HEAD = 128
KEYS = PROMPT + RESP
EPSILON = 1e-06
SCALE = HEAD ** (-0.5)
LOG2E = 1.4426950408889634
SHARP = SCALE * LOG2E
MASKED = -1e30
MESH = pl.DeviceIdType.MESH
F32 = jnp.float32
BF16 = jnp.bfloat16
NT = (((1,), (1,)), ((), ()))


def dot_nn(a, b):
    return jnp.dot(a, b, preferred_element_type=F32)


def dot_nt(a, b):
    return lax.dot_general(a, b, NT, preferred_element_type=F32)


def normed_rows(rows):
    wide = rows.astype(F32)
    inverse = lax.rsqrt(jnp.mean(wide * wide, axis=1, keepdims=True) + EPSILON)
    return wide, inverse


def softmax_columns(blocks, keep):
    top = functools.reduce(jnp.maximum, [jnp.max(b, axis=0, keepdims=True) for b in blocks])
    shift = top * SHARP
    raised = [jnp.exp2(b * SHARP - shift) for b in blocks]
    total = functools.reduce(jnp.add, [jnp.sum(b, axis=0, keepdims=True) for b in raised])
    factor = keep / total
    return [b * factor for b in raised]


def score_gradient(probs, weights, p_grads):
    inner = functools.reduce(
        jnp.add,
        [
            jnp.sum(w.astype(F32) * g, axis=0, keepdims=True)
            for w, g in zip(weights, p_grads, strict=True)
        ],
    )
    return [(p * (g - inner)).astype(BF16) for p, g in zip(probs, p_grads, strict=True)]


def kernel(
    heads,
    groups,
    n_dp,
    n_tensor,
    plen,
    rlen,
    rown,
    qg,
    kg,
    q_hbm,
    k_hbm,
    v_hbm,
    o_hbm,
    dqv,
    dk_out,
    dv_out,
    gains_out,
    qv,
    ov,
    length_at,
    kself,
    vself,
    near_k0,
    near_k1,
    near_v0,
    near_v1,
    eye,
    gain_col,
    bias_lower,
    bias_upper,
    bias_own,
    kn_p,
    knt_p,
    dk_acc,
    dv_acc,
    qg_acc,
    kg_acc,
    r_o,
    r_qt,
    r_qnt,
    r_inv,
    r_k,
    r_kt,
    r_khat,
    r_p,
    back,
    back_sib,
    back_r4,
    back_r2,
    back_o4,
    back_o2,
    part_a,
    part_b,
    buf_a,
    buf_b,
    known,
    load_sem,
    fwd_send,
    fwd_recv,
    bwd_send,
    bwd_recv,
    a_send,
    a_recv,
    b_send,
    b_recv,
):
    dp = lax.axis_index("dp")
    tensor = lax.axis_index("tensor")
    core = lax.rem(dp, 2)
    up = (lax.rem(dp + 2, n_dp), tensor)
    down = (lax.rem(dp + n_dp - 2, n_dp), tensor)
    sibling = (dp + 1 - 2 * core, tensor)
    near = (near_k0, near_k1, near_v0, near_v1)
    chunks = 2 * heads

    columns = n_dp // 16
    n_a = columns * n_tensor
    place_a = lax.div(dp, 16) * n_tensor + tensor
    place_b = lax.rem(dp, 16)

    def within(at, size):
        return jnp.where(at < size, at, at - size)

    column = lax.div(dp, 16)
    peers_a = []
    for i in range(columns):
        for j in range(n_tensor):
            if i or j:
                at, side = within(column + i, columns), within(tensor + j, n_tensor)
                peers_a.append((at * n_tensor + side, (at * 16 + place_b, side)))
    peers_b = []
    for k in range(1, 16):
        at = within(place_b + k, 16)
        peers_b.append((at, (dp - place_b + at, tensor)))

    def cols(h, g=None):
        if g is None:
            return pl.ds(h * HEAD, HEAD)
        return pl.ds(pl.multiple_of((h * groups + g) * HEAD, HEAD), HEAD)

    barrier = pltpu.get_barrier_semaphore()
    rings = [
        (dp - place_b + within(place_b + 2, 16), tensor),
        (dp - place_b + within(place_b + 14, 16), tensor),
    ]
    if n_tensor > 1:
        rings += [(dp, within(tensor + j, n_tensor)) for j in (1, n_tensor - 1)]
    if columns > 1:
        rings += [(within(column + i, columns) * 16 + place_b, tensor) for i in (1, columns - 1)]
    greeted = [up, down, sibling] + rings
    for device in greeted:
        pl.semaphore_signal(barrier, inc=1, device_id=device, device_id_type=MESH)

    loads = []

    def load(src, dst):
        copy = pltpu.make_async_copy(src, dst, load_sem.at[len(loads)])
        copy.start()
        loads.append(copy)
        return copy

    staged = []
    for c in range(chunks):
        h = c % heads
        source = (k_hbm if c < heads else v_hbm).at[pl.ds(0, PROMPT), cols(h)]
        staged.append(load(source, near[c].at[0, pl.ds(0, PROMPT)]))
    load_length = load(plen, length_at)
    load_k = load(k_hbm, kself)
    wide = groups * HEAD
    load_q, load_o = [], []
    for h in range(heads):
        load_q.append(load(q_hbm.at[:, pl.ds(h * wide, wide)], qv.at[:, pl.ds(h * wide, wide)]))
        load_o.append(load(o_hbm.at[:, pl.ds(h * wide, wide)], ov.at[:, pl.ds(h * wide, wide)]))
        if h == 0:
            load_v = load(v_hbm, vself)

    load_length.wait()
    length = length_at[0]
    query_at = lax.rem(lax.broadcasted_iota(jnp.int32, (1, PROMPT), 1), PROMPT // 2)
    keep_lower = (query_at < length).astype(F32)
    keep_upper = (query_at + PROMPT // 2 < length).astype(F32)
    near_k0[0, pl.ds(PROMPT, 16)] = jnp.full((16, HEAD), length.astype(F32)).astype(BF16)

    def prepare():
        row_at = lax.broadcasted_iota(jnp.int32, (HEAD, HEAD), 0)
        col_at = lax.broadcasted_iota(jnp.int32, (HEAD, HEAD), 1)
        eye[...] = jnp.where(row_at == col_at, 1.0, 0.0).astype(BF16)
        gain_col[...] = jnp.broadcast_to(qg[...], (HEAD, HEAD)).T
        for lower, bias in ((True, bias_lower), (False, bias_upper)):
            key_at = lax.broadcasted_iota(jnp.int32, bias.shape, 0)
            query_at = lax.rem(lax.broadcasted_iota(jnp.int32, bias.shape, 1), PROMPT // 2)
            query_at = query_at if lower else query_at + PROMPT // 2
            bias[...] = jnp.where((key_at <= query_at) & (key_at < length), 0.0, MASKED)
        own_key = lax.broadcasted_iota(jnp.int32, (RESP, HEAD), 0)
        own_query = lax.rem(lax.broadcasted_iota(jnp.int32, (RESP, HEAD), 1), RESP)
        bias_own[...] = jnp.where(own_key <= own_query, 0.0, MASKED)
        qg_acc[...] = jnp.zeros_like(qg_acc)
        kg_acc[...] = jnp.zeros_like(kg_acc)
        dk_acc[...] = jnp.zeros_like(dk_acc)
        dv_acc[...] = jnp.zeros_like(dv_acc)

    picks = [jnp.clip(lax.rem(dp + n_dp - rown[s], n_dp), 1, 4) for s in range(2)]

    for copy in staged:
        copy.wait()
    pl.semaphore_wait(barrier, len(greeted))

    def tell(turn):
        for i, device in enumerate(rings):
            pl.semaphore_signal(
                known.at[turn, i], inc=1, device_id=device, device_id_type=MESH
            )

    def hear(turn):
        for i in range(len(rings)):
            pl.semaphore_wait(known.at[turn, i], 1)

    def slot(c, d):
        return near[c].at[d]

    def forward(kind, c, src, dst, device):
        return pltpu.make_async_remote_copy(
            src_ref=slot(c, src),
            dst_ref=slot(c, dst),
            send_sem=fwd_send.at[kind, c],
            recv_sem=fwd_recv.at[kind, c],
            device_id=device,
            device_id_type=MESH,
        )

    def hop(c):
        return forward(0, c, 0, 2, up)

    def relay(c):
        return forward(1, c, 2, 4, up)

    def across(c, far, src):
        return forward(2 + far, c, src, 1 + 2 * far, sibling)

    def send_own(c):
        hop(c).start()

        @pl.when(core == 0)
        def _():
            across(c, 0, 0).start()

    def pass_on(c):
        hop(c).wait_recv()
        relay(c).start()

        @pl.when(core == 0)
        def _():
            across(c, 1, 2).start()

        @pl.when(core == 1)
        def _():
            across(c, 0, 2).start()

    def arrive(c):
        relay(c).wait_recv()

        @pl.when(core == 1)
        def _():
            across(c, 1, 4).start()

        across(c, 0, 0).wait_recv()
        across(c, 1, 0).wait_recv()

    def prepared(rows):
        qt = dot_nt(eye[...], rows)
        inverse = lax.rsqrt(jnp.mean(qt * qt, axis=0, keepdims=True) + EPSILON)
        gain = jnp.concatenate([gain_col[...]] * (qt.shape[1] // HEAD), axis=1)
        return qt, inverse, (qt * inverse * gain).astype(BF16)

    def query_backward(grad, qt, inverse):
        gain = jnp.concatenate([gain_col[...]] * (qt.shape[1] // HEAD), axis=1)
        both = grad * qt
        mean = jnp.mean(both * gain, axis=0, keepdims=True)
        scaled = inverse * SCALE
        out = grad * gain * scaled - qt * (inverse * inverse * scaled * mean)
        portion = both * scaled
        portion = sum(portion[:, at : at + HEAD] for at in range(0, qt.shape[1], HEAD))
        return out.T.astype(BF16), portion

    def prepare_prompt_keys(h):
        wide_k, inverse = normed_rows(kself[pl.ds(0, PROMPT), cols(h)])
        normed = (wide_k * inverse * kg[...]).astype(BF16)
        kn_p[h] = normed
        knt_p[h] = dot_nt(eye[...], normed).astype(BF16)

    half = PROMPT // 2

    def prompt_half(h, pairs):
        lo, hi = pl.ds(0, half), pl.ds(half, half)
        parts = []
        for pair in pairs:
            at = [cols(h, 2 * pair + i) for i in range(2)]
            parts.append((at, lo, lo, bias_lower, keep_lower))
            parts.append((at, hi, pl.ds(0, PROMPT), bias_upper, keep_upper))
        stacked = [jnp.concatenate([qv[r, a] for a in at], axis=0) for at, r, *_ in parts]
        ready = [prepared(x) for x in stacked]
        rows_o = [jnp.concatenate([ov[r, a] for a in at], axis=0) for at, r, *_ in parts]
        p_grad = [dot_nt(vself[p[2], cols(h)], x) for p, x in zip(parts, rows_o)]
        scores = [dot_nn(kn_p[h, p[2]], r[2]) + p[3][...] for p, r in zip(parts, ready)]
        probs = [softmax_columns([x], p[4])[0] for p, x in zip(parts, scores)]
        weights = [p.astype(BF16) for p in probs]
        s_grad = [score_gradient([p], [w], [g])[0] for p, w, g in zip(probs, weights, p_grad)]
        grad = [dot_nn(knt_p[h, :, p[2]], x) for p, x in zip(parts, s_grad)]
        dv = [dot_nn(w, x) for w, x in zip(weights, rows_o)]
        dk = [dot_nt(x, r[2]) for x, r in zip(s_grad, ready)]
        for total, terms in ((dv_acc, dv), (dk_acc, dk)):
            total[h, lo] += sum(terms[0::2]) + sum(t[:half] for t in terms[1::2])
            total[h, hi] += sum(t[half:] for t in terms[1::2])
        portions = []
        for p, x, g in zip(parts, ready, grad):
            out, portion = query_backward(g, x[0], x[1])
            portions.append(portion)
            for i, a in enumerate(p[0]):
                dqv[p[1], a] = out[i * half : (i + 1) * half]
        qg_acc[...] += sum(portions)

    def response_rows(s):
        return pl.ds(PROMPT + s * RESP, RESP)

    def prepare_responses(h):
        ready = []
        for s in range(2):
            rows = response_rows(s)
            stacked = jnp.concatenate([qv[rows, cols(h, g)] for g in range(groups)], axis=0)
            r_o[h, s] = jnp.concatenate([ov[rows, cols(h, g)] for g in range(groups)], axis=0)
            ready.append(prepared(stacked))
        for s, (qt, inverse, qnt) in enumerate(ready):
            r_qt[h, s] = qt
            r_qnt[h, s] = qnt
            r_inv[h, s] = jnp.broadcast_to(inverse, (8, inverse.shape[1]))
            wide_k, inverse = normed_rows(kself[response_rows(s), cols(h)])
            hat = wide_k * inverse
            r_khat[h, s, pl.ds(PROMPT, RESP)] = hat
            r_k[h, s, pl.ds(PROMPT, RESP)] = (hat * kg[...]).astype(BF16)

    span = 2 * HEAD
    firsts = range(0, groups * RESP, span)
    blocks = [(s, pl.ds(first, span), first) for s in range(2) for first in firsts]

    def response_keys(h):
        normed, bias, keep = [], [], []
        for s in range(2):
            wide_k, inverse = normed_rows(near[h][picks[s], pl.ds(0, PROMPT)])
            hat = wide_k * inverse
            r_khat[h, s, pl.ds(0, PROMPT)] = hat
            r_k[h, s, pl.ds(0, PROMPT)] = (hat * kg[...]).astype(BF16)
            normed.append(r_k[h, s])
            owner_length = near_k0[picks[s], pl.ds(PROMPT, 16)].astype(F32)[0:1]
            at = lax.broadcasted_iota(jnp.int32, (PROMPT, HEAD), 0).astype(F32)
            seen = jnp.where(at < owner_length, 0.0, MASKED)
            seen = jnp.concatenate([seen, bias_own[...]], axis=0)
            bias.append(jnp.concatenate([seen, seen], axis=1))
            place = lax.rem(lax.broadcasted_iota(jnp.int32, (1, span), 1), RESP)
            keep.append((place < rlen[s]).astype(F32))
        scores = [dot_nn(normed[s], r_qnt[h, s, :, b]) + bias[s] for s, b, _ in blocks]
        probs = [softmax_columns([x], keep[s])[0] for (s, _, _), x in zip(blocks, scores)]
        weights = [p.astype(BF16) for p in probs]
        terms = [dot_nn(w, r_o[h, s, b]) for (s, b, _), w in zip(blocks, weights)]
        for (s, b, _), p in zip(blocks, probs):
            r_p[h, s, :, b] = p
        half_way = len(terms) // 2
        totals = [sum(terms[:half_way]), sum(terms[half_way:])]
        give_back(heads + h, totals)
        for s in range(2):
            dv_out[response_rows(s), cols(h)] = totals[s][PROMPT:].astype(BF16)
            r_kt[h, s] = dot_nt(eye[...], normed[s]).astype(BF16)

    def response_values(h):
        rows_v = [
            jnp.concatenate([near[heads + h][picks[s]], vself[response_rows(s), cols(h)]], axis=0)
            for s in range(2)
        ]
        p_grad = [dot_nt(rows_v[s], r_o[h, s, b]) for s, b, _ in blocks]
        probs = [r_p[h, s, :, b] for s, b, _ in blocks]
        s_grad = [score_gradient([p], [p.astype(BF16)], [g])[0] for p, g in zip(probs, p_grad)]
        terms = [dot_nt(x, r_qnt[h, s, :, b]) for (s, b, _), x in zip(blocks, s_grad)]
        half_way = len(terms) // 2
        totals = [sum(terms[:half_way]), sum(terms[half_way:])]
        give_back(h, totals)
        grads = [dot_nn(r_kt[h, s], x) for (s, _, _), x in zip(blocks, s_grad)]
        portions = []
        for (s, b, first), grad in zip(blocks, grads):
            out, portion = query_backward(grad, r_qt[h, s, :, b], r_inv[h, s, 0:1, b])
            portions.append(portion)
            for i in range(span // RESP):
                dqv[response_rows(s), cols(h, first // RESP + i)] = out[i * RESP : (i + 1) * RESP]
        qg_acc[...] += sum(portions)
        portion = sum(totals[s] * r_khat[h, s] for s in range(2)) * SCALE
        kg_acc[...] += jnp.sum(portion.reshape(KEYS // 8, 8, HEAD), axis=0)
        for s in range(2):
            rows = response_rows(s)
            dk_out[rows, cols(h)] = key_backward(totals[s][PROMPT:], kself[rows, cols(h)])

    def key_backward(grad, rows):
        wide_k, inverse = normed_rows(rows)
        scaled = grad * kg[...]
        mean = jnp.mean(scaled * wide_k, axis=1, keepdims=True)
        factor = inverse * SCALE
        return (scaled * factor - wide_k * (inverse * inverse * factor * mean)).astype(BF16)

    def backward(kind, c, src, dst, device):
        return pltpu.make_async_remote_copy(
            src_ref=src,
            dst_ref=dst,
            send_sem=bwd_send.at[kind, c],
            recv_sem=bwd_recv.at[kind, c],
            device_id=device,
            device_id_type=MESH,
        )

    def back_across(c):
        return backward(0, c, back.at[c, pl.ds(0, 2)], back_sib.at[c], sibling)

    def back_far(c):
        return backward(1, c, back_o4.at[c], back_r4.at[c], down)

    def back_near(c):
        return backward(2, c, back_o2.at[c], back_r2.at[c], down)

    def give_back(c, terms):
        for i, distance in enumerate((1, 3, 2, 4)):
            chosen = [(pick == distance).astype(F32) for pick in picks]
            term = chosen[0] * terms[0][:PROMPT] + chosen[1] * terms[1][:PROMPT]
            back[c, i] = term.astype(BF16)
        back_across(c).start()

    upper = core.astype(F32)

    def give_back_far(c):
        back_across(c).wait_recv()
        total = back[c, 3].astype(F32) + upper * back_sib[c, 1].astype(F32)
        back_o4[c] = total.astype(BF16)
        back_far(c).start()

    def give_back_near(c):
        back_far(c).wait_recv()
        other = upper * back_sib[c, 0].astype(F32) + (1.0 - upper) * back_sib[c, 1].astype(F32)
        total = back[c, 2].astype(F32) + back_r4[c].astype(F32) + other
        back_o2[c] = total.astype(BF16)
        back_near(c).start()

    def taken_back(c):
        back_near(c).wait_recv()
        return back_r2[c].astype(F32) + (1.0 - upper) * back_sib[c, 0].astype(F32)

    def exchange(peers, place, source, buffer, send_sem, recv_sem):
        def copy(other, device, slot):
            return pltpu.make_async_remote_copy(
                src_ref=source,
                dst_ref=buffer.at[slot],
                send_sem=send_sem.at[other],
                recv_sem=recv_sem.at[slot],
                device_id=device,
                device_id_type=MESH,
            )

        def start():
            for other, device in peers:
                copy(other, device, place).start()
            buffer[place] = source[...]

        def collect():
            for other, device in peers:
                copy(other, device, other).wait_recv()
            total = buffer[0]
            for i in range(1, len(peers) + 1):
                total = total + buffer[i]
            return total

        def finish():
            for other, device in peers:
                copy(other, device, place).wait_send()

        return start, collect, finish

    start_a, collect_a, finish_a = exchange(peers_b, place_b, part_b, buf_b, b_send, b_recv)
    start_b, collect_b, finish_b = exchange(peers_a, place_a, part_a, buf_a, a_send, a_recv)

    def prompt_key_portion():
        for h in range(heads):
            wide_k, inverse = normed_rows(kself[pl.ds(0, PROMPT), cols(h)])
            portion = dk_acc[h] * (wide_k * inverse) * SCALE
            kg_acc[...] += jnp.sum(portion.reshape(PROMPT // 8, 8, HEAD), axis=0)

    def sum_gains():
        part_b[...] = jnp.concatenate(
            [
                jnp.sum(qg_acc[...].T, axis=0, keepdims=True),
                jnp.sum(kg_acc[...], axis=0, keepdims=True),
                jnp.zeros((6, HEAD), F32),
            ],
            axis=0,
        )

    prompt = pl.ds(0, PROMPT)

    def finish_values(h):
        dv_out[prompt, cols(h)] = (dv_acc[h] + taken_back(heads + h)).astype(BF16)

    def finish_keys(h):
        total = dk_acc[h] + taken_back(h)
        dk_out[prompt, cols(h)] = key_backward(total, kself[prompt, cols(h)])

    first, second = range(groups // 4), range(groups // 4, groups // 2)
    send_own(0)
    tell(0)
    prepare()
    load_k.wait()
    load_v.wait()
    for h in range(heads):
        load_q[h].wait()
        load_o[h].wait()
        prepare_prompt_keys(h)
        prepare_responses(h)
    send_own(1)
    prompt_half(0, first)
    send_own(2)
    prompt_half(0, second)
    hear(0)
    tell(1)
    prompt_half(1, first)
    pass_on(0)
    send_own(3)
    prompt_half(1, second)
    hear(1)
    tell(2)
    pass_on(1)
    prompt_key_portion()
    pass_on(2)
    pass_on(3)
    hear(2)
    tell(3)
    arrive(0)
    response_keys(0)
    arrive(1)
    response_keys(1)
    give_back_far(2)
    arrive(2)
    response_values(0)
    give_back_far(3)
    arrive(3)
    response_values(1)
    sum_gains()
    hear(3)
    start_a()
    give_back_far(0)
    give_back_far(1)
    give_back_near(2)
    give_back_near(3)
    part_a[...] = collect_a()
    start_b()
    give_back_near(0)
    give_back_near(1)
    for h in range(heads):
        finish_values(h)
    for h in range(heads):
        finish_keys(h)
    gains_out[...] = collect_b()

    finish_a()
    finish_b()
    for c in range(chunks):
        hop(c).wait_send()
        relay(c).wait_send()
        across(c, 0, 0).wait_send()
        across(c, 1, 0).wait_send()
        back_across(c).wait_send()
        back_far(c).wait_send()
        back_near(c).wait_send()


def hand_out(q, k, v, gains, q_out, k_out, v_out, qg_out, kg_out, sems):
    copies = [
        pltpu.make_async_copy(src, dst, sems.at[i])
        for i, (src, dst) in enumerate(
            [
                *[(q.at[r], q_out.at[r]) for r in (pl.ds(96 * i, 96) for i in range(4))],
                (k, k_out),
                (v, v_out),
                (gains.at[0:1], qg_out),
                (gains.at[1:2], kg_out),
            ]
        )
    ]
    for copy in copies:
        copy.start()
    for copy in copies:
        copy.wait()


def on_device(
    n_dp, n_tensor, queries, keys, values, output_gradient, q_gain, k_gain, prompt_len, resp_len, resp_owner
):
    heads = keys.shape[1] // HEAD
    groups = queries.shape[1] // keys.shape[1]
    rows = queries.shape[0]
    chunks = 2 * heads
    n_a = n_dp // 16 * n_tensor
    vmem = pl.BlockSpec(memory_space=pltpu.VMEM)
    smem = pl.BlockSpec(memory_space=pltpu.SMEM)
    hbm = pl.BlockSpec(memory_space=pltpu.HBM)
    asked = groups * RESP
    scratch = [
        pltpu.VMEM(queries.shape, BF16),
        pltpu.VMEM(queries.shape, BF16),
        pltpu.SMEM((1,), jnp.int32),
        pltpu.VMEM(keys.shape, BF16),
        pltpu.VMEM(keys.shape, BF16),
        pltpu.VMEM((5, PROMPT + 16, HEAD), BF16),
        pltpu.VMEM((5, PROMPT, HEAD), BF16),
        pltpu.VMEM((5, PROMPT, HEAD), BF16),
        pltpu.VMEM((5, PROMPT, HEAD), BF16),
        pltpu.VMEM((HEAD, HEAD), BF16),
        pltpu.VMEM((HEAD, HEAD), F32),
        pltpu.VMEM((PROMPT // 2, PROMPT), F32),
        pltpu.VMEM((PROMPT, PROMPT), F32),
        pltpu.VMEM((RESP, HEAD), F32),
        pltpu.VMEM((heads, PROMPT, HEAD), BF16),
        pltpu.VMEM((heads, HEAD, PROMPT), BF16),
        pltpu.VMEM((heads, PROMPT, HEAD), F32),
        pltpu.VMEM((heads, PROMPT, HEAD), F32),
        pltpu.VMEM((HEAD, HEAD), F32),
        pltpu.VMEM((8, HEAD), F32),
        pltpu.VMEM((heads, 2, asked, HEAD), BF16),
        pltpu.VMEM((heads, 2, HEAD, asked), F32),
        pltpu.VMEM((heads, 2, HEAD, asked), BF16),
        pltpu.VMEM((heads, 2, 8, asked), F32),
        pltpu.VMEM((heads, 2, KEYS, HEAD), BF16),
        pltpu.VMEM((heads, 2, HEAD, KEYS), BF16),
        pltpu.VMEM((heads, 2, KEYS, HEAD), F32),
        pltpu.VMEM((heads, 2, KEYS, asked), F32),
        pltpu.VMEM((chunks, 4, PROMPT, HEAD), BF16),
        pltpu.VMEM((chunks, 2, PROMPT, HEAD), BF16),
        pltpu.VMEM((chunks, PROMPT, HEAD), BF16),
        pltpu.VMEM((chunks, PROMPT, HEAD), BF16),
        pltpu.VMEM((chunks, PROMPT, HEAD), BF16),
        pltpu.VMEM((chunks, PROMPT, HEAD), BF16),
        pltpu.VMEM((8, HEAD), F32),
        pltpu.VMEM((8, HEAD), F32),
        pltpu.VMEM((n_a, 8, HEAD), F32),
        pltpu.VMEM((16, 8, HEAD), F32),
        pltpu.SemaphoreType.REGULAR((4, 6)),
        pltpu.SemaphoreType.DMA((chunks + 3 + 2 * heads,)),
        pltpu.SemaphoreType.DMA((4, chunks)),
        pltpu.SemaphoreType.DMA((4, chunks)),
        pltpu.SemaphoreType.DMA((3, chunks)),
        pltpu.SemaphoreType.DMA((3, chunks)),
        pltpu.SemaphoreType.DMA((n_a,)),
        pltpu.SemaphoreType.DMA((n_a,)),
        pltpu.SemaphoreType.DMA((16,)),
        pltpu.SemaphoreType.DMA((16,)),
    ]
    results = pl.pallas_call(
        functools.partial(kernel, heads, groups, n_dp, n_tensor),
        out_shape=(
            pltpu.VMEM(queries.shape, BF16),
            pltpu.VMEM(keys.shape, BF16),
            pltpu.VMEM(keys.shape, BF16),
            pltpu.VMEM((8, HEAD), F32),
        ),
        in_specs=[hbm, smem, smem, vmem, vmem, hbm, hbm, hbm, hbm],
        out_specs=(vmem, vmem, vmem, vmem),
        scratch_shapes=scratch,
        compiler_params=pltpu.CompilerParams(
            collective_id=0, has_side_effects=True, vmem_limit_bytes=56 * 2**20
        ),
        name="attention",
    )(
        prompt_len,
        resp_len,
        resp_owner,
        q_gain.reshape(1, HEAD),
        k_gain.reshape(1, HEAD),
        *[
            pltpu.with_memory_space_constraint(a, pltpu.HBM)
            for a in (queries, keys, values, output_gradient)
        ],
    )
    q_grad, k_grad, v_grad, q_gain_grad, k_gain_grad = pl.pallas_call(
        hand_out,
        out_shape=(
            jax.ShapeDtypeStruct(queries.shape, BF16),
            jax.ShapeDtypeStruct(keys.shape, BF16),
            jax.ShapeDtypeStruct(keys.shape, BF16),
            jax.ShapeDtypeStruct((1, HEAD), F32),
            jax.ShapeDtypeStruct((1, HEAD), F32),
        ),
        in_specs=[vmem] * 4,
        out_specs=(hbm,) * 5,
        scratch_shapes=[pltpu.SemaphoreType.DMA((8,))],
        compiler_params=pltpu.CompilerParams(vmem_limit_bytes=16 * 2**20),
        name="hand_out",
    )(*[pltpu.with_memory_space_constraint(x, pltpu.VMEM) for x in results])
    return q_grad, k_grad, v_grad, q_gain_grad.reshape(HEAD), k_gain_grad.reshape(HEAD)


def solution(mesh):
    rows, whole = P("dp", "tensor"), P()
    return jax.shard_map(
        functools.partial(on_device, mesh.shape["dp"], mesh.shape["tensor"]),
        mesh=mesh,
        in_specs=(rows, rows, rows, rows, whole, whole, P("dp"), P("dp"), P("dp")),
        out_specs=(rows, rows, rows, whole, whole),
        check_vma=False,
    )
```

```python
import functools

import jax
import jax.numpy as jnp
from jax import lax
from jax.experimental import pallas as pl
from jax.experimental.pallas import tpu as pltpu
from jax.sharding import PartitionSpec as P

PROMPT = 256
RESP = 64
HEAD = 128
KEYS = PROMPT + RESP
EPSILON = 1e-06
SCALE = HEAD ** (-0.5)
LOG2E = 1.4426950408889634
SHARP = SCALE * LOG2E
MASKED = -1e30
MESH = pl.DeviceIdType.MESH
F32 = jnp.float32
BF16 = jnp.bfloat16
NT = (((1,), (1,)), ((), ()))


def dot_nn(a, b):
    return jnp.dot(a, b, preferred_element_type=F32)


def dot_nt(a, b):
    return lax.dot_general(a, b, NT, preferred_element_type=F32)


def normed_rows(rows):
    wide = rows.astype(F32)
    inverse = lax.rsqrt(jnp.mean(wide * wide, axis=1, keepdims=True) + EPSILON)
    return wide, inverse


def softmax_columns(blocks, keep):
    top = functools.reduce(jnp.maximum, [jnp.max(b, axis=0, keepdims=True) for b in blocks])
    shift = top * SHARP
    raised = [jnp.exp2(b * SHARP - shift) for b in blocks]
    total = functools.reduce(jnp.add, [jnp.sum(b, axis=0, keepdims=True) for b in raised])
    factor = keep / total
    return [b * factor for b in raised]


def score_gradient(probs, weights, p_grads):
    inner = functools.reduce(
        jnp.add,
        [
            jnp.sum(w.astype(F32) * g, axis=0, keepdims=True)
            for w, g in zip(weights, p_grads, strict=True)
        ],
    )
    return [(p * (g - inner)).astype(BF16) for p, g in zip(probs, p_grads, strict=True)]


def kernel(
    heads,
    groups,
    n_dp,
    n_tensor,
    plen,
    rlen,
    rown,
    qg,
    kg,
    q_hbm,
    k_hbm,
    v_hbm,
    o_hbm,
    dqv,
    dk_out,
    dv_out,
    gains_out,
    qv,
    ov,
    length_at,
    kself,
    vself,
    near_k0,
    near_k1,
    near_v0,
    near_v1,
    eye,
    gain_col,
    bias_lower,
    bias_upper,
    bias_own,
    kn_p,
    knt_p,
    dk_acc,
    dv_acc,
    qg_acc,
    kg_acc,
    r_o,
    r_qt,
    r_qnt,
    r_inv,
    r_k,
    r_kt,
    r_khat,
    r_p,
    back,
    back_sib,
    back_r4,
    back_r2,
    back_o4,
    back_o2,
    part_a,
    part_b,
    buf_a,
    buf_b,
    known,
    load_sem,
    fwd_send,
    fwd_recv,
    bwd_send,
    bwd_recv,
    a_send,
    a_recv,
    b_send,
    b_recv,
):
    dp = lax.axis_index("dp")
    tensor = lax.axis_index("tensor")
    core = lax.rem(dp, 2)
    up = (lax.rem(dp + 2, n_dp), tensor)
    down = (lax.rem(dp + n_dp - 2, n_dp), tensor)
    sibling = (dp + 1 - 2 * core, tensor)
    near = (near_k0, near_k1, near_v0, near_v1)
    chunks = 2 * heads

    columns = n_dp // 16
    n_a = columns * n_tensor
    place_a = lax.div(dp, 16) * n_tensor + tensor
    place_b = lax.rem(dp, 16)

    def within(at, size):
        return jnp.where(at < size, at, at - size)

    column = lax.div(dp, 16)
    peers_a = []
    for i in range(columns):
        for j in range(n_tensor):
            if i or j:
                at, side = within(column + i, columns), within(tensor + j, n_tensor)
                peers_a.append((at * n_tensor + side, (at * 16 + place_b, side)))
    peers_b = []
    for k in range(1, 16):
        at = within(place_b + k, 16)
        peers_b.append((at, (dp - place_b + at, tensor)))

    def cols(h, g=None):
        if g is None:
            return pl.ds(h * HEAD, HEAD)
        return pl.ds(pl.multiple_of((h * groups + g) * HEAD, HEAD), HEAD)

    barrier = pltpu.get_barrier_semaphore()
    rings = [
        (dp - place_b + within(place_b + 2, 16), tensor),
        (dp - place_b + within(place_b + 14, 16), tensor),
    ]
    if n_tensor > 1:
        rings += [(dp, within(tensor + j, n_tensor)) for j in (1, n_tensor - 1)]
    if columns > 1:
        rings += [(within(column + i, columns) * 16 + place_b, tensor) for i in (1, columns - 1)]
    greeted = [up, down, sibling] + rings
    for device in greeted:
        pl.semaphore_signal(barrier, inc=1, device_id=device, device_id_type=MESH)

    loads = []

    def load(src, dst):
        copy = pltpu.make_async_copy(src, dst, load_sem.at[len(loads)])
        copy.start()
        loads.append(copy)
        return copy

    staged = []
    for c in range(chunks):
        h = c % heads
        source = (k_hbm if c < heads else v_hbm).at[pl.ds(0, PROMPT), cols(h)]
        staged.append(load(source, near[c].at[0, pl.ds(0, PROMPT)]))
    load_length = load(plen, length_at)
    load_k = load(k_hbm, kself)
    wide = groups * HEAD
    load_q, load_o = [], []
    for h in range(heads):
        load_q.append(load(q_hbm.at[:, pl.ds(h * wide, wide)], qv.at[:, pl.ds(h * wide, wide)]))
        load_o.append(load(o_hbm.at[:, pl.ds(h * wide, wide)], ov.at[:, pl.ds(h * wide, wide)]))
        if h == 0:
            load_v = load(v_hbm, vself)

    load_length.wait()
    length = length_at[0]
    query_at = lax.rem(lax.broadcasted_iota(jnp.int32, (1, PROMPT), 1), PROMPT // 2)
    keep_lower = (query_at < length).astype(F32)
    keep_upper = (query_at + PROMPT // 2 < length).astype(F32)
    near_k0[0, pl.ds(PROMPT, 16)] = jnp.full((16, HEAD), length.astype(F32)).astype(BF16)

    def prepare():
        row_at = lax.broadcasted_iota(jnp.int32, (HEAD, HEAD), 0)
        col_at = lax.broadcasted_iota(jnp.int32, (HEAD, HEAD), 1)
        eye[...] = jnp.where(row_at == col_at, 1.0, 0.0).astype(BF16)
        gain_col[...] = jnp.broadcast_to(qg[...], (HEAD, HEAD)).T
        for lower, bias in ((True, bias_lower), (False, bias_upper)):
            key_at = lax.broadcasted_iota(jnp.int32, bias.shape, 0)
            query_at = lax.rem(lax.broadcasted_iota(jnp.int32, bias.shape, 1), PROMPT // 2)
            query_at = query_at if lower else query_at + PROMPT // 2
            bias[...] = jnp.where((key_at <= query_at) & (key_at < length), 0.0, MASKED)
        own_key = lax.broadcasted_iota(jnp.int32, (RESP, HEAD), 0)
        own_query = lax.rem(lax.broadcasted_iota(jnp.int32, (RESP, HEAD), 1), RESP)
        bias_own[...] = jnp.where(own_key <= own_query, 0.0, MASKED)
        qg_acc[...] = jnp.zeros_like(qg_acc)
        kg_acc[...] = jnp.zeros_like(kg_acc)
        dk_acc[...] = jnp.zeros_like(dk_acc)
        dv_acc[...] = jnp.zeros_like(dv_acc)

    picks = [jnp.clip(lax.rem(dp + n_dp - rown[s], n_dp), 1, 4) for s in range(2)]

    for copy in staged:
        copy.wait()
    pl.semaphore_wait(barrier, len(greeted))

    def tell(turn):
        for i, device in enumerate(rings):
            pl.semaphore_signal(
                known.at[turn, i], inc=1, device_id=device, device_id_type=MESH
            )

    def hear(turn):
        for i in range(len(rings)):
            pl.semaphore_wait(known.at[turn, i], 1)

    def slot(c, d):
        return near[c].at[d]

    def forward(kind, c, src, dst, device):
        return pltpu.make_async_remote_copy(
            src_ref=slot(c, src),
            dst_ref=slot(c, dst),
            send_sem=fwd_send.at[kind, c],
            recv_sem=fwd_recv.at[kind, c],
            device_id=device,
            device_id_type=MESH,
        )

    def hop(c):
        return forward(0, c, 0, 2, up)

    def relay(c):
        return forward(1, c, 2, 4, up)

    def across(c, far, src):
        return forward(2 + far, c, src, 1 + 2 * far, sibling)

    def send_own(c):
        hop(c).start()

        @pl.when(core == 0)
        def _():
            across(c, 0, 0).start()

    def pass_on(c):
        hop(c).wait_recv()
        relay(c).start()

        @pl.when(core == 0)
        def _():
            across(c, 1, 2).start()

        @pl.when(core == 1)
        def _():
            across(c, 0, 2).start()

    def arrive(c):
        relay(c).wait_recv()

        @pl.when(core == 1)
        def _():
            across(c, 1, 4).start()

        across(c, 0, 0).wait_recv()
        across(c, 1, 0).wait_recv()

    def prepared(rows):
        qt = dot_nt(eye[...], rows)
        inverse = lax.rsqrt(jnp.mean(qt * qt, axis=0, keepdims=True) + EPSILON)
        gain = jnp.concatenate([gain_col[...]] * (qt.shape[1] // HEAD), axis=1)
        return qt, inverse, (qt * inverse * gain).astype(BF16)

    def query_backward(grad, qt, inverse):
        gain = jnp.concatenate([gain_col[...]] * (qt.shape[1] // HEAD), axis=1)
        both = grad * qt
        mean = jnp.mean(both * gain, axis=0, keepdims=True)
        scaled = inverse * SCALE
        out = grad * gain * scaled - qt * (inverse * inverse * scaled * mean)
        portion = both * scaled
        portion = sum(portion[:, at : at + HEAD] for at in range(0, qt.shape[1], HEAD))
        return out.T.astype(BF16), portion

    def prepare_prompt_keys(h):
        wide_k, inverse = normed_rows(kself[pl.ds(0, PROMPT), cols(h)])
        normed = (wide_k * inverse * kg[...]).astype(BF16)
        kn_p[h] = normed
        knt_p[h] = dot_nt(eye[...], normed).astype(BF16)

    half = PROMPT // 2

    def prompt_half(h, pairs):
        lo, hi = pl.ds(0, half), pl.ds(half, half)
        parts = []
        for pair in pairs:
            at = [cols(h, 2 * pair + i) for i in range(2)]
            parts.append((at, lo, lo, bias_lower, keep_lower))
            parts.append((at, hi, pl.ds(0, PROMPT), bias_upper, keep_upper))
        stacked = [jnp.concatenate([qv[r, a] for a in at], axis=0) for at, r, *_ in parts]
        ready = [prepared(x) for x in stacked]
        rows_o = [jnp.concatenate([ov[r, a] for a in at], axis=0) for at, r, *_ in parts]
        p_grad = [dot_nt(vself[p[2], cols(h)], x) for p, x in zip(parts, rows_o)]
        scores = [dot_nn(kn_p[h, p[2]], r[2]) + p[3][...] for p, r in zip(parts, ready)]
        probs = [softmax_columns([x], p[4])[0] for p, x in zip(parts, scores)]
        weights = [p.astype(BF16) for p in probs]
        s_grad = [score_gradient([p], [w], [g])[0] for p, w, g in zip(probs, weights, p_grad)]
        grad = [dot_nn(knt_p[h, :, p[2]], x) for p, x in zip(parts, s_grad)]
        dv = [dot_nn(w, x) for w, x in zip(weights, rows_o)]
        dk = [dot_nt(x, r[2]) for x, r in zip(s_grad, ready)]
        for total, terms in ((dv_acc, dv), (dk_acc, dk)):
            total[h, lo] += sum(terms[0::2]) + sum(t[:half] for t in terms[1::2])
            total[h, hi] += sum(t[half:] for t in terms[1::2])
        portions = []
        for p, x, g in zip(parts, ready, grad):
            out, portion = query_backward(g, x[0], x[1])
            portions.append(portion)
            for i, a in enumerate(p[0]):
                dqv[p[1], a] = out[i * half : (i + 1) * half]
        qg_acc[...] += sum(portions)

    def response_rows(s):
        return pl.ds(PROMPT + s * RESP, RESP)

    def prepare_responses(h):
        ready = []
        for s in range(2):
            rows = response_rows(s)
            stacked = jnp.concatenate([qv[rows, cols(h, g)] for g in range(groups)], axis=0)
            r_o[h, s] = jnp.concatenate([ov[rows, cols(h, g)] for g in range(groups)], axis=0)
            ready.append(prepared(stacked))
        for s, (qt, inverse, qnt) in enumerate(ready):
            r_qt[h, s] = qt
            r_qnt[h, s] = qnt
            r_inv[h, s] = jnp.broadcast_to(inverse, (8, inverse.shape[1]))
            wide_k, inverse = normed_rows(kself[response_rows(s), cols(h)])
            hat = wide_k * inverse
            r_khat[h, s, pl.ds(PROMPT, RESP)] = hat
            r_k[h, s, pl.ds(PROMPT, RESP)] = (hat * kg[...]).astype(BF16)

    span = 2 * HEAD
    firsts = range(0, groups * RESP, span)
    blocks = [(s, pl.ds(first, span), first) for s in range(2) for first in firsts]

    def response_keys(h):
        normed, bias, keep = [], [], []
        for s in range(2):
            wide_k, inverse = normed_rows(near[h][picks[s], pl.ds(0, PROMPT)])
            hat = wide_k * inverse
            r_khat[h, s, pl.ds(0, PROMPT)] = hat
            r_k[h, s, pl.ds(0, PROMPT)] = (hat * kg[...]).astype(BF16)
            normed.append(r_k[h, s])
            owner_length = near_k0[picks[s], pl.ds(PROMPT, 16)].astype(F32)[0:1]
            at = lax.broadcasted_iota(jnp.int32, (PROMPT, HEAD), 0).astype(F32)
            seen = jnp.where(at < owner_length, 0.0, MASKED)
            seen = jnp.concatenate([seen, bias_own[...]], axis=0)
            bias.append(jnp.concatenate([seen, seen], axis=1))
            place = lax.rem(lax.broadcasted_iota(jnp.int32, (1, span), 1), RESP)
            keep.append((place < rlen[s]).astype(F32))
        scores = [dot_nn(normed[s], r_qnt[h, s, :, b]) + bias[s] for s, b, _ in blocks]
        probs = [softmax_columns([x], keep[s])[0] for (s, _, _), x in zip(blocks, scores)]
        weights = [p.astype(BF16) for p in probs]
        terms = [dot_nn(w, r_o[h, s, b]) for (s, b, _), w in zip(blocks, weights)]
        for (s, b, _), p in zip(blocks, probs):
            r_p[h, s, :, b] = p
        half_way = len(terms) // 2
        totals = [sum(terms[:half_way]), sum(terms[half_way:])]
        give_back(heads + h, totals)
        for s in range(2):
            dv_out[response_rows(s), cols(h)] = totals[s][PROMPT:].astype(BF16)
            r_kt[h, s] = dot_nt(eye[...], normed[s]).astype(BF16)

    def response_values(h):
        rows_v = [
            jnp.concatenate([near[heads + h][picks[s]], vself[response_rows(s), cols(h)]], axis=0)
            for s in range(2)
        ]
        p_grad = [dot_nt(rows_v[s], r_o[h, s, b]) for s, b, _ in blocks]
        probs = [r_p[h, s, :, b] for s, b, _ in blocks]
        s_grad = [score_gradient([p], [p.astype(BF16)], [g])[0] for p, g in zip(probs, p_grad)]
        terms = [dot_nt(x, r_qnt[h, s, :, b]) for (s, b, _), x in zip(blocks, s_grad)]
        half_way = len(terms) // 2
        totals = [sum(terms[:half_way]), sum(terms[half_way:])]
        give_back(h, totals)
        grads = [dot_nn(r_kt[h, s], x) for (s, _, _), x in zip(blocks, s_grad)]
        portions = []
        for (s, b, first), grad in zip(blocks, grads):
            out, portion = query_backward(grad, r_qt[h, s, :, b], r_inv[h, s, 0:1, b])
            portions.append(portion)
            for i in range(span // RESP):
                dqv[response_rows(s), cols(h, first // RESP + i)] = out[i * RESP : (i + 1) * RESP]
        qg_acc[...] += sum(portions)
        portion = sum(totals[s] * r_khat[h, s] for s in range(2)) * SCALE
        kg_acc[...] += jnp.sum(portion.reshape(KEYS // 8, 8, HEAD), axis=0)
        for s in range(2):
            rows = response_rows(s)
            dk_out[rows, cols(h)] = key_backward(totals[s][PROMPT:], kself[rows, cols(h)])

    def key_backward(grad, rows):
        wide_k, inverse = normed_rows(rows)
        scaled = grad * kg[...]
        mean = jnp.mean(scaled * wide_k, axis=1, keepdims=True)
        factor = inverse * SCALE
        return (scaled * factor - wide_k * (inverse * inverse * factor * mean)).astype(BF16)

    def backward(kind, c, src, dst, device):
        return pltpu.make_async_remote_copy(
            src_ref=src,
            dst_ref=dst,
            send_sem=bwd_send.at[kind, c],
            recv_sem=bwd_recv.at[kind, c],
            device_id=device,
            device_id_type=MESH,
        )

    def back_across(c):
        return backward(0, c, back.at[c, pl.ds(0, 2)], back_sib.at[c], sibling)

    def back_far(c):
        return backward(1, c, back_o4.at[c], back_r4.at[c], down)

    def back_near(c):
        return backward(2, c, back_o2.at[c], back_r2.at[c], down)

    def give_back(c, terms):
        for i, distance in enumerate((1, 3, 2, 4)):
            chosen = [(pick == distance).astype(F32) for pick in picks]
            term = chosen[0] * terms[0][:PROMPT] + chosen[1] * terms[1][:PROMPT]
            back[c, i] = term.astype(BF16)
        back_across(c).start()

    upper = core.astype(F32)

    def give_back_far(c):
        back_across(c).wait_recv()
        total = back[c, 3].astype(F32) + upper * back_sib[c, 1].astype(F32)
        back_o4[c] = total.astype(BF16)
        back_far(c).start()

    def give_back_near(c):
        back_far(c).wait_recv()
        other = upper * back_sib[c, 0].astype(F32) + (1.0 - upper) * back_sib[c, 1].astype(F32)
        total = back[c, 2].astype(F32) + back_r4[c].astype(F32) + other
        back_o2[c] = total.astype(BF16)
        back_near(c).start()

    def taken_back(c):
        back_near(c).wait_recv()
        return back_r2[c].astype(F32) + (1.0 - upper) * back_sib[c, 0].astype(F32)

    def exchange(peers, place, source, buffer, send_sem, recv_sem):
        def copy(other, device, slot):
            return pltpu.make_async_remote_copy(
                src_ref=source,
                dst_ref=buffer.at[slot],
                send_sem=send_sem.at[other],
                recv_sem=recv_sem.at[slot],
                device_id=device,
                device_id_type=MESH,
            )

        def start():
            for other, device in peers:
                copy(other, device, place).start()
            buffer[place] = source[...]

        def collect():
            for other, device in peers:
                copy(other, device, other).wait_recv()
            total = buffer[0]
            for i in range(1, len(peers) + 1):
                total = total + buffer[i]
            return total

        def finish():
            for other, device in peers:
                copy(other, device, place).wait_send()

        return start, collect, finish

    start_a, collect_a, finish_a = exchange(peers_b, place_b, part_b, buf_b, b_send, b_recv)
    start_b, collect_b, finish_b = exchange(peers_a, place_a, part_a, buf_a, a_send, a_recv)

    def prompt_key_portion():
        for h in range(heads):
            wide_k, inverse = normed_rows(kself[pl.ds(0, PROMPT), cols(h)])
            portion = dk_acc[h] * (wide_k * inverse) * SCALE
            kg_acc[...] += jnp.sum(portion.reshape(PROMPT // 8, 8, HEAD), axis=0)

    def sum_gains():
        part_b[...] = jnp.concatenate(
            [
                jnp.sum(qg_acc[...].T, axis=0, keepdims=True),
                jnp.sum(kg_acc[...], axis=0, keepdims=True),
                jnp.zeros((6, HEAD), F32),
            ],
            axis=0,
        )

    prompt = pl.ds(0, PROMPT)

    def finish_values(h):
        dv_out[prompt, cols(h)] = (dv_acc[h] + taken_back(heads + h)).astype(BF16)

    def finish_keys(h):
        total = dk_acc[h] + taken_back(h)
        dk_out[prompt, cols(h)] = key_backward(total, kself[prompt, cols(h)])

    first, second = range(groups // 4), range(groups // 4, groups // 2)
    for c in range(chunks):
        send_own(c)
    tell(0)
    prepare()
    load_k.wait()
    load_v.wait()
    for h in range(heads):
        load_q[h].wait()
        load_o[h].wait()
        prepare_prompt_keys(h)
        prepare_responses(h)
    prompt_half(0, first)
    prompt_half(0, second)
    hear(0)
    tell(1)
    prompt_half(1, first)
    pass_on(0)
    prompt_half(1, second)
    hear(1)
    tell(2)
    pass_on(1)
    prompt_key_portion()
    pass_on(2)
    pass_on(3)
    hear(2)
    tell(3)
    arrive(0)
    response_keys(0)
    arrive(1)
    response_keys(1)
    give_back_far(2)
    arrive(2)
    response_values(0)
    give_back_far(3)
    arrive(3)
    response_values(1)
    sum_gains()
    hear(3)
    start_a()
    give_back_far(0)
    give_back_far(1)
    give_back_near(2)
    give_back_near(3)
    part_a[...] = collect_a()
    start_b()
    give_back_near(0)
    give_back_near(1)
    for h in range(heads):
        finish_values(h)
    for h in range(heads):
        finish_keys(h)
    gains_out[...] = collect_b()

    finish_a()
    finish_b()
    for c in range(chunks):
        hop(c).wait_send()
        relay(c).wait_send()
        across(c, 0, 0).wait_send()
        across(c, 1, 0).wait_send()
        back_across(c).wait_send()
        back_far(c).wait_send()
        back_near(c).wait_send()


def hand_out(q, k, v, gains, q_out, k_out, v_out, qg_out, kg_out, sems):
    copies = [
        pltpu.make_async_copy(src, dst, sems.at[i])
        for i, (src, dst) in enumerate(
            [
                *[(q.at[r], q_out.at[r]) for r in (pl.ds(96 * i, 96) for i in range(4))],
                (k, k_out),
                (v, v_out),
                (gains.at[0:1], qg_out),
                (gains.at[1:2], kg_out),
            ]
        )
    ]
    for copy in copies:
        copy.start()
    for copy in copies:
        copy.wait()


def on_device(
    n_dp, n_tensor, queries, keys, values, output_gradient, q_gain, k_gain, prompt_len, resp_len, resp_owner
):
    heads = keys.shape[1] // HEAD
    groups = queries.shape[1] // keys.shape[1]
    rows = queries.shape[0]
    chunks = 2 * heads
    n_a = n_dp // 16 * n_tensor
    vmem = pl.BlockSpec(memory_space=pltpu.VMEM)
    smem = pl.BlockSpec(memory_space=pltpu.SMEM)
    hbm = pl.BlockSpec(memory_space=pltpu.HBM)
    asked = groups * RESP
    scratch = [
        pltpu.VMEM(queries.shape, BF16),
        pltpu.VMEM(queries.shape, BF16),
        pltpu.SMEM((1,), jnp.int32),
        pltpu.VMEM(keys.shape, BF16),
        pltpu.VMEM(keys.shape, BF16),
        pltpu.VMEM((5, PROMPT + 16, HEAD), BF16),
        pltpu.VMEM((5, PROMPT, HEAD), BF16),
        pltpu.VMEM((5, PROMPT, HEAD), BF16),
        pltpu.VMEM((5, PROMPT, HEAD), BF16),
        pltpu.VMEM((HEAD, HEAD), BF16),
        pltpu.VMEM((HEAD, HEAD), F32),
        pltpu.VMEM((PROMPT // 2, PROMPT), F32),
        pltpu.VMEM((PROMPT, PROMPT), F32),
        pltpu.VMEM((RESP, HEAD), F32),
        pltpu.VMEM((heads, PROMPT, HEAD), BF16),
        pltpu.VMEM((heads, HEAD, PROMPT), BF16),
        pltpu.VMEM((heads, PROMPT, HEAD), F32),
        pltpu.VMEM((heads, PROMPT, HEAD), F32),
        pltpu.VMEM((HEAD, HEAD), F32),
        pltpu.VMEM((8, HEAD), F32),
        pltpu.VMEM((heads, 2, asked, HEAD), BF16),
        pltpu.VMEM((heads, 2, HEAD, asked), F32),
        pltpu.VMEM((heads, 2, HEAD, asked), BF16),
        pltpu.VMEM((heads, 2, 8, asked), F32),
        pltpu.VMEM((heads, 2, KEYS, HEAD), BF16),
        pltpu.VMEM((heads, 2, HEAD, KEYS), BF16),
        pltpu.VMEM((heads, 2, KEYS, HEAD), F32),
        pltpu.VMEM((heads, 2, KEYS, asked), F32),
        pltpu.VMEM((chunks, 4, PROMPT, HEAD), BF16),
        pltpu.VMEM((chunks, 2, PROMPT, HEAD), BF16),
        pltpu.VMEM((chunks, PROMPT, HEAD), BF16),
        pltpu.VMEM((chunks, PROMPT, HEAD), BF16),
        pltpu.VMEM((chunks, PROMPT, HEAD), BF16),
        pltpu.VMEM((chunks, PROMPT, HEAD), BF16),
        pltpu.VMEM((8, HEAD), F32),
        pltpu.VMEM((8, HEAD), F32),
        pltpu.VMEM((n_a, 8, HEAD), F32),
        pltpu.VMEM((16, 8, HEAD), F32),
        pltpu.SemaphoreType.REGULAR((4, 6)),
        pltpu.SemaphoreType.DMA((chunks + 3 + 2 * heads,)),
        pltpu.SemaphoreType.DMA((4, chunks)),
        pltpu.SemaphoreType.DMA((4, chunks)),
        pltpu.SemaphoreType.DMA((3, chunks)),
        pltpu.SemaphoreType.DMA((3, chunks)),
        pltpu.SemaphoreType.DMA((n_a,)),
        pltpu.SemaphoreType.DMA((n_a,)),
        pltpu.SemaphoreType.DMA((16,)),
        pltpu.SemaphoreType.DMA((16,)),
    ]
    results = pl.pallas_call(
        functools.partial(kernel, heads, groups, n_dp, n_tensor),
        out_shape=(
            pltpu.VMEM(queries.shape, BF16),
            pltpu.VMEM(keys.shape, BF16),
            pltpu.VMEM(keys.shape, BF16),
            pltpu.VMEM((8, HEAD), F32),
        ),
        in_specs=[hbm, smem, smem, vmem, vmem, hbm, hbm, hbm, hbm],
        out_specs=(vmem, vmem, vmem, vmem),
        scratch_shapes=scratch,
        compiler_params=pltpu.CompilerParams(
            collective_id=0, has_side_effects=True, vmem_limit_bytes=56 * 2**20
        ),
        name="attention",
    )(
        prompt_len,
        resp_len,
        resp_owner,
        q_gain.reshape(1, HEAD),
        k_gain.reshape(1, HEAD),
        *[
            pltpu.with_memory_space_constraint(a, pltpu.HBM)
            for a in (queries, keys, values, output_gradient)
        ],
    )
    q_grad, k_grad, v_grad, q_gain_grad, k_gain_grad = pl.pallas_call(
        hand_out,
        out_shape=(
            jax.ShapeDtypeStruct(queries.shape, BF16),
            jax.ShapeDtypeStruct(keys.shape, BF16),
            jax.ShapeDtypeStruct(keys.shape, BF16),
            jax.ShapeDtypeStruct((1, HEAD), F32),
            jax.ShapeDtypeStruct((1, HEAD), F32),
        ),
        in_specs=[vmem] * 4,
        out_specs=(hbm,) * 5,
        scratch_shapes=[pltpu.SemaphoreType.DMA((8,))],
        compiler_params=pltpu.CompilerParams(vmem_limit_bytes=16 * 2**20),
        name="hand_out",
    )(*[pltpu.with_memory_space_constraint(x, pltpu.VMEM) for x in results])
    return q_grad, k_grad, v_grad, q_gain_grad.reshape(HEAD), k_gain_grad.reshape(HEAD)


def solution(mesh):
    rows, whole = P("dp", "tensor"), P()
    return jax.shard_map(
        functools.partial(on_device, mesh.shape["dp"], mesh.shape["tensor"]),
        mesh=mesh,
        in_specs=(rows, rows, rows, rows, whole, whole, P("dp"), P("dp"), P("dp")),
        out_specs=(rows, rows, rows, whole, whole),
        check_vma=False,
    )
```

```python
import functools

import jax
import jax.numpy as jnp
from jax import lax
from jax.experimental import pallas as pl
from jax.experimental.pallas import tpu as pltpu
from jax.sharding import PartitionSpec as P

PROMPT = 256
RESP = 64
HEAD = 128
KEYS = PROMPT + RESP
EPSILON = 1e-06
SCALE = HEAD ** (-0.5)
LOG2E = 1.4426950408889634
SHARP = SCALE * LOG2E
MASKED = -1e30
MESH = pl.DeviceIdType.MESH
F32 = jnp.float32
BF16 = jnp.bfloat16
NT = (((1,), (1,)), ((), ()))


def dot_nn(a, b):
    return jnp.dot(a, b, preferred_element_type=F32)


def dot_nt(a, b):
    return lax.dot_general(a, b, NT, preferred_element_type=F32)


def normed_rows(rows):
    wide = rows.astype(F32)
    inverse = lax.rsqrt(jnp.mean(wide * wide, axis=1, keepdims=True) + EPSILON)
    return wide, inverse


def softmax_columns(blocks, keep):
    top = functools.reduce(jnp.maximum, [jnp.max(b, axis=0, keepdims=True) for b in blocks])
    shift = top * SHARP
    raised = [jnp.exp2(b * SHARP - shift) for b in blocks]
    total = functools.reduce(jnp.add, [jnp.sum(b, axis=0, keepdims=True) for b in raised])
    factor = keep / total
    return [b * factor for b in raised]


def score_gradient(probs, weights, p_grads):
    inner = functools.reduce(
        jnp.add,
        [
            jnp.sum(w.astype(F32) * g, axis=0, keepdims=True)
            for w, g in zip(weights, p_grads, strict=True)
        ],
    )
    return [(p * (g - inner)).astype(BF16) for p, g in zip(probs, p_grads, strict=True)]


def kernel(
    heads,
    groups,
    n_dp,
    n_tensor,
    plen,
    rlen,
    rown,
    qg,
    kg,
    q_hbm,
    k_hbm,
    v_hbm,
    o_hbm,
    dqv,
    dk_out,
    dv_out,
    gains_out,
    qv,
    ov,
    length_at,
    kself,
    vself,
    near_k0,
    near_k1,
    near_v0,
    near_v1,
    eye,
    gain_col,
    bias_lower,
    bias_upper,
    bias_own,
    kn_p,
    knt_p,
    dk_acc,
    dv_acc,
    qg_acc,
    kg_acc,
    r_o,
    r_qt,
    r_qnt,
    r_inv,
    r_k,
    r_kt,
    r_khat,
    r_p,
    back,
    back_sib,
    back_r4,
    back_r2,
    back_o4,
    back_o2,
    part_a,
    part_b,
    buf_a,
    buf_b,
    known,
    load_sem,
    fwd_send,
    fwd_recv,
    bwd_send,
    bwd_recv,
    a_send,
    a_recv,
    b_send,
    b_recv,
):
    dp = lax.axis_index("dp")
    tensor = lax.axis_index("tensor")
    core = lax.rem(dp, 2)
    up = (lax.rem(dp + 2, n_dp), tensor)
    down = (lax.rem(dp + n_dp - 2, n_dp), tensor)
    sibling = (dp + 1 - 2 * core, tensor)
    near = (near_k0, near_k1, near_v0, near_v1)
    chunks = 2 * heads

    columns = n_dp // 16
    n_a = columns * n_tensor
    place_a = lax.div(dp, 16) * n_tensor + tensor
    place_b = lax.rem(dp, 16)

    def within(at, size):
        return jnp.where(at < size, at, at - size)

    column = lax.div(dp, 16)
    peers_a = []
    for i in range(columns):
        for j in range(n_tensor):
            if i or j:
                at, side = within(column + i, columns), within(tensor + j, n_tensor)
                peers_a.append((at * n_tensor + side, (at * 16 + place_b, side)))
    peers_b = []
    for k in range(1, 16):
        at = within(place_b + k, 16)
        peers_b.append((at, (dp - place_b + at, tensor)))

    def cols(h, g=None):
        if g is None:
            return pl.ds(h * HEAD, HEAD)
        return pl.ds(pl.multiple_of((h * groups + g) * HEAD, HEAD), HEAD)

    barrier = pltpu.get_barrier_semaphore()
    rings = [
        (dp - place_b + within(place_b + 2, 16), tensor),
        (dp - place_b + within(place_b + 14, 16), tensor),
    ]
    if n_tensor > 1:
        rings += [(dp, within(tensor + j, n_tensor)) for j in (1, n_tensor - 1)]
    if columns > 1:
        rings += [(within(column + i, columns) * 16 + place_b, tensor) for i in (1, columns - 1)]
    greeted = [up, down, sibling] + rings
    for device in greeted:
        pl.semaphore_signal(barrier, inc=1, device_id=device, device_id_type=MESH)

    loads = []

    def load(src, dst):
        copy = pltpu.make_async_copy(src, dst, load_sem.at[len(loads)])
        copy.start()
        loads.append(copy)
        return copy

    staged = []
    for c in range(chunks):
        h = c % heads
        source = (k_hbm if c < heads else v_hbm).at[pl.ds(0, PROMPT), cols(h)]
        staged.append(load(source, near[c].at[0, pl.ds(0, PROMPT)]))
    load_length = load(plen, length_at)
    load_k = load(k_hbm, kself)
    wide = groups * HEAD
    load_q, load_o = [], []
    for h in range(heads):
        load_q.append(load(q_hbm.at[:, pl.ds(h * wide, wide)], qv.at[:, pl.ds(h * wide, wide)]))
        load_o.append(load(o_hbm.at[:, pl.ds(h * wide, wide)], ov.at[:, pl.ds(h * wide, wide)]))
        if h == 0:
            load_v = load(v_hbm, vself)

    load_length.wait()
    length = length_at[0]
    query_at = lax.rem(lax.broadcasted_iota(jnp.int32, (1, PROMPT), 1), PROMPT // 2)
    keep_lower = (query_at < length).astype(F32)
    keep_upper = (query_at + PROMPT // 2 < length).astype(F32)
    near_k0[0, pl.ds(PROMPT, 16)] = jnp.full((16, HEAD), length.astype(F32)).astype(BF16)

    def prepare():
        row_at = lax.broadcasted_iota(jnp.int32, (HEAD, HEAD), 0)
        col_at = lax.broadcasted_iota(jnp.int32, (HEAD, HEAD), 1)
        eye[...] = jnp.where(row_at == col_at, 1.0, 0.0).astype(BF16)
        gain_col[...] = jnp.broadcast_to(qg[...], (HEAD, HEAD)).T
        for lower, bias in ((True, bias_lower), (False, bias_upper)):
            key_at = lax.broadcasted_iota(jnp.int32, bias.shape, 0)
            query_at = lax.rem(lax.broadcasted_iota(jnp.int32, bias.shape, 1), PROMPT // 2)
            query_at = query_at if lower else query_at + PROMPT // 2
            bias[...] = jnp.where((key_at <= query_at) & (key_at < length), 0.0, MASKED)
        own_key = lax.broadcasted_iota(jnp.int32, (RESP, HEAD), 0)
        own_query = lax.rem(lax.broadcasted_iota(jnp.int32, (RESP, HEAD), 1), RESP)
        bias_own[...] = jnp.where(own_key <= own_query, 0.0, MASKED)
        qg_acc[...] = jnp.zeros_like(qg_acc)
        kg_acc[...] = jnp.zeros_like(kg_acc)
        dk_acc[...] = jnp.zeros_like(dk_acc)
        dv_acc[...] = jnp.zeros_like(dv_acc)

    picks = [jnp.clip(lax.rem(dp + n_dp - rown[s], n_dp), 1, 4) for s in range(2)]

    for copy in staged:
        copy.wait()
    pl.semaphore_wait(barrier, len(greeted))

    def tell(turn):
        for i, device in enumerate(rings):
            pl.semaphore_signal(
                known.at[turn, i], inc=1, device_id=device, device_id_type=MESH
            )

    def hear(turn):
        for i in range(len(rings)):
            pl.semaphore_wait(known.at[turn, i], 1)

    def slot(c, d):
        return near[c].at[d]

    def forward(kind, c, src, dst, device):
        return pltpu.make_async_remote_copy(
            src_ref=slot(c, src),
            dst_ref=slot(c, dst),
            send_sem=fwd_send.at[kind, c],
            recv_sem=fwd_recv.at[kind, c],
            device_id=device,
            device_id_type=MESH,
        )

    def hop(c):
        return forward(0, c, 0, 2, up)

    def relay(c):
        return forward(1, c, 2, 4, up)

    def across(c, far, src):
        return forward(2 + far, c, src, 1 + 2 * far, sibling)

    def send_own(c):
        hop(c).start()

        @pl.when(core == 0)
        def _():
            across(c, 0, 0).start()

    def pass_on(c):
        hop(c).wait_recv()
        relay(c).start()

        @pl.when(core == 0)
        def _():
            across(c, 1, 2).start()

        @pl.when(core == 1)
        def _():
            across(c, 0, 2).start()

    def arrive(c):
        relay(c).wait_recv()

        @pl.when(core == 1)
        def _():
            across(c, 1, 4).start()

        across(c, 0, 0).wait_recv()
        across(c, 1, 0).wait_recv()

    def prepared(rows):
        qt = dot_nt(eye[...], rows)
        inverse = lax.rsqrt(jnp.mean(qt * qt, axis=0, keepdims=True) + EPSILON)
        gain = jnp.concatenate([gain_col[...]] * (qt.shape[1] // HEAD), axis=1)
        return qt, inverse, (qt * inverse * gain).astype(BF16)

    def query_backward(grad, qt, inverse):
        gain = jnp.concatenate([gain_col[...]] * (qt.shape[1] // HEAD), axis=1)
        both = grad * qt
        mean = jnp.mean(both * gain, axis=0, keepdims=True)
        scaled = inverse * SCALE
        out = grad * gain * scaled - qt * (inverse * inverse * scaled * mean)
        portion = both * scaled
        portion = sum(portion[:, at : at + HEAD] for at in range(0, qt.shape[1], HEAD))
        return out.T.astype(BF16), portion

    def prepare_prompt_keys(h):
        wide_k, inverse = normed_rows(kself[pl.ds(0, PROMPT), cols(h)])
        normed = (wide_k * inverse * kg[...]).astype(BF16)
        kn_p[h] = normed
        knt_p[h] = dot_nt(eye[...], normed).astype(BF16)

    half = PROMPT // 2

    def prompt_half(h, pairs):
        lo, hi = pl.ds(0, half), pl.ds(half, half)
        parts = []
        for pair in pairs:
            at = [cols(h, 2 * pair + i) for i in range(2)]
            parts.append((at, lo, lo, bias_lower, keep_lower))
            parts.append((at, hi, pl.ds(0, PROMPT), bias_upper, keep_upper))
        stacked = [jnp.concatenate([qv[r, a] for a in at], axis=0) for at, r, *_ in parts]
        ready = [prepared(x) for x in stacked]
        rows_o = [jnp.concatenate([ov[r, a] for a in at], axis=0) for at, r, *_ in parts]
        p_grad = [dot_nt(vself[p[2], cols(h)], x) for p, x in zip(parts, rows_o)]
        scores = [dot_nn(kn_p[h, p[2]], r[2]) + p[3][...] for p, r in zip(parts, ready)]
        probs = [softmax_columns([x], p[4])[0] for p, x in zip(parts, scores)]
        weights = [p.astype(BF16) for p in probs]
        s_grad = [score_gradient([p], [w], [g])[0] for p, w, g in zip(probs, weights, p_grad)]
        grad = [dot_nn(knt_p[h, :, p[2]], x) for p, x in zip(parts, s_grad)]
        dv = [dot_nn(w, x) for w, x in zip(weights, rows_o)]
        dk = [dot_nt(x, r[2]) for x, r in zip(s_grad, ready)]
        for total, terms in ((dv_acc, dv), (dk_acc, dk)):
            total[h, lo] += sum(terms[0::2]) + sum(t[:half] for t in terms[1::2])
            total[h, hi] += sum(t[half:] for t in terms[1::2])
        portions = []
        for p, x, g in zip(parts, ready, grad):
            out, portion = query_backward(g, x[0], x[1])
            portions.append(portion)
            for i, a in enumerate(p[0]):
                dqv[p[1], a] = out[i * half : (i + 1) * half]
        qg_acc[...] += sum(portions)

    def response_rows(s):
        return pl.ds(PROMPT + s * RESP, RESP)

    def prepare_responses(h):
        ready = []
        for s in range(2):
            rows = response_rows(s)
            stacked = jnp.concatenate([qv[rows, cols(h, g)] for g in range(groups)], axis=0)
            r_o[h, s] = jnp.concatenate([ov[rows, cols(h, g)] for g in range(groups)], axis=0)
            ready.append(prepared(stacked))
        for s, (qt, inverse, qnt) in enumerate(ready):
            r_qt[h, s] = qt
            r_qnt[h, s] = qnt
            r_inv[h, s] = jnp.broadcast_to(inverse, (8, inverse.shape[1]))
            wide_k, inverse = normed_rows(kself[response_rows(s), cols(h)])
            hat = wide_k * inverse
            r_khat[h, s, pl.ds(PROMPT, RESP)] = hat
            r_k[h, s, pl.ds(PROMPT, RESP)] = (hat * kg[...]).astype(BF16)

    span = 2 * HEAD
    firsts = range(0, groups * RESP, span)
    blocks = [(s, pl.ds(first, span), first) for s in range(2) for first in firsts]

    def response_keys(h):
        normed, bias, keep = [], [], []
        for s in range(2):
            wide_k, inverse = normed_rows(near[h][picks[s], pl.ds(0, PROMPT)])
            hat = wide_k * inverse
            r_khat[h, s, pl.ds(0, PROMPT)] = hat
            r_k[h, s, pl.ds(0, PROMPT)] = (hat * kg[...]).astype(BF16)
            normed.append(r_k[h, s])
            owner_length = near_k0[picks[s], pl.ds(PROMPT, 16)].astype(F32)[0:1]
            at = lax.broadcasted_iota(jnp.int32, (PROMPT, HEAD), 0).astype(F32)
            seen = jnp.where(at < owner_length, 0.0, MASKED)
            seen = jnp.concatenate([seen, bias_own[...]], axis=0)
            bias.append(jnp.concatenate([seen, seen], axis=1))
            place = lax.rem(lax.broadcasted_iota(jnp.int32, (1, span), 1), RESP)
            keep.append((place < rlen[s]).astype(F32))
        scores = [dot_nn(normed[s], r_qnt[h, s, :, b]) + bias[s] for s, b, _ in blocks]
        probs = [softmax_columns([x], keep[s])[0] for (s, _, _), x in zip(blocks, scores)]
        weights = [p.astype(BF16) for p in probs]
        terms = [dot_nn(w, r_o[h, s, b]) for (s, b, _), w in zip(blocks, weights)]
        for (s, b, _), p in zip(blocks, probs):
            r_p[h, s, :, b] = p
        half_way = len(terms) // 2
        totals = [sum(terms[:half_way]), sum(terms[half_way:])]
        give_back(heads + h, totals)
        for s in range(2):
            dv_out[response_rows(s), cols(h)] = totals[s][PROMPT:].astype(BF16)
            r_kt[h, s] = dot_nt(eye[...], normed[s]).astype(BF16)

    def response_values(h):
        rows_v = [
            jnp.concatenate([near[heads + h][picks[s]], vself[response_rows(s), cols(h)]], axis=0)
            for s in range(2)
        ]
        p_grad = [dot_nt(rows_v[s], r_o[h, s, b]) for s, b, _ in blocks]
        probs = [r_p[h, s, :, b] for s, b, _ in blocks]
        s_grad = [score_gradient([p], [p.astype(BF16)], [g])[0] for p, g in zip(probs, p_grad)]
        terms = [dot_nt(x, r_qnt[h, s, :, b]) for (s, b, _), x in zip(blocks, s_grad)]
        half_way = len(terms) // 2
        totals = [sum(terms[:half_way]), sum(terms[half_way:])]
        give_back(h, totals)
        grads = [dot_nn(r_kt[h, s], x) for (s, _, _), x in zip(blocks, s_grad)]
        portions = []
        for (s, b, first), grad in zip(blocks, grads):
            out, portion = query_backward(grad, r_qt[h, s, :, b], r_inv[h, s, 0:1, b])
            portions.append(portion)
            for i in range(span // RESP):
                dqv[response_rows(s), cols(h, first // RESP + i)] = out[i * RESP : (i + 1) * RESP]
        qg_acc[...] += sum(portions)
        portion = sum(totals[s] * r_khat[h, s] for s in range(2)) * SCALE
        kg_acc[...] += jnp.sum(portion.reshape(KEYS // 8, 8, HEAD), axis=0)
        for s in range(2):
            rows = response_rows(s)
            dk_out[rows, cols(h)] = key_backward(totals[s][PROMPT:], kself[rows, cols(h)])

    def key_backward(grad, rows):
        wide_k, inverse = normed_rows(rows)
        scaled = grad * kg[...]
        mean = jnp.mean(scaled * wide_k, axis=1, keepdims=True)
        factor = inverse * SCALE
        return (scaled * factor - wide_k * (inverse * inverse * factor * mean)).astype(BF16)

    def backward(kind, c, src, dst, device):
        return pltpu.make_async_remote_copy(
            src_ref=src,
            dst_ref=dst,
            send_sem=bwd_send.at[kind, c],
            recv_sem=bwd_recv.at[kind, c],
            device_id=device,
            device_id_type=MESH,
        )

    def back_across(c):
        return backward(0, c, back.at[c, pl.ds(0, 2)], back_sib.at[c], sibling)

    def back_far(c):
        return backward(1, c, back_o4.at[c], back_r4.at[c], down)

    def back_near(c):
        return backward(2, c, back_o2.at[c], back_r2.at[c], down)

    def give_back(c, terms):
        for i, distance in enumerate((1, 3, 2, 4)):
            chosen = [(pick == distance).astype(F32) for pick in picks]
            term = chosen[0] * terms[0][:PROMPT] + chosen[1] * terms[1][:PROMPT]
            back[c, i] = term.astype(BF16)
        back_across(c).start()

    upper = core.astype(F32)

    def give_back_far(c):
        back_across(c).wait_recv()
        total = back[c, 3].astype(F32) + upper * back_sib[c, 1].astype(F32)
        back_o4[c] = total.astype(BF16)
        back_far(c).start()

    def give_back_near(c):
        back_far(c).wait_recv()
        other = upper * back_sib[c, 0].astype(F32) + (1.0 - upper) * back_sib[c, 1].astype(F32)
        total = back[c, 2].astype(F32) + back_r4[c].astype(F32) + other
        back_o2[c] = total.astype(BF16)
        back_near(c).start()

    def taken_back(c):
        back_near(c).wait_recv()
        return back_r2[c].astype(F32) + (1.0 - upper) * back_sib[c, 0].astype(F32)

    def exchange(peers, place, source, buffer, send_sem, recv_sem):
        def copy(other, device, slot):
            return pltpu.make_async_remote_copy(
                src_ref=source,
                dst_ref=buffer.at[slot],
                send_sem=send_sem.at[other],
                recv_sem=recv_sem.at[slot],
                device_id=device,
                device_id_type=MESH,
            )

        def start():
            for other, device in peers:
                copy(other, device, place).start()
            buffer[place] = source[...]

        def collect():
            for other, device in peers:
                copy(other, device, other).wait_recv()
            total = buffer[0]
            for i in range(1, len(peers) + 1):
                total = total + buffer[i]
            return total

        def finish():
            for other, device in peers:
                copy(other, device, place).wait_send()

        return start, collect, finish

    start_a, collect_a, finish_a = exchange(peers_b, place_b, part_b, buf_b, b_send, b_recv)
    start_b, collect_b, finish_b = exchange(peers_a, place_a, part_a, buf_a, a_send, a_recv)

    def prompt_key_portion():
        for h in range(heads):
            wide_k, inverse = normed_rows(kself[pl.ds(0, PROMPT), cols(h)])
            portion = dk_acc[h] * (wide_k * inverse) * SCALE
            kg_acc[...] += jnp.sum(portion.reshape(PROMPT // 8, 8, HEAD), axis=0)

    def sum_gains():
        part_b[...] = jnp.concatenate(
            [
                jnp.sum(qg_acc[...].T, axis=0, keepdims=True),
                jnp.sum(kg_acc[...], axis=0, keepdims=True),
                jnp.zeros((6, HEAD), F32),
            ],
            axis=0,
        )

    prompt = pl.ds(0, PROMPT)

    def finish_values(h):
        dv_out[prompt, cols(h)] = (dv_acc[h] + taken_back(heads + h)).astype(BF16)

    def finish_keys(h):
        total = dk_acc[h] + taken_back(h)
        dk_out[prompt, cols(h)] = key_backward(total, kself[prompt, cols(h)])

    first, second = range(groups // 4), range(groups // 4, groups // 2)
    for c in range(chunks):
        send_own(c)
    tell(0)
    prepare()
    load_k.wait()
    load_v.wait()
    for h in range(heads):
        load_q[h].wait()
        load_o[h].wait()
        prepare_prompt_keys(h)
        prepare_responses(h)
    prompt_half(0, first)
    prompt_half(0, second)
    hear(0)
    tell(1)
    prompt_half(1, first)
    pass_on(0)
    prompt_half(1, second)
    hear(1)
    tell(2)
    pass_on(1)
    prompt_key_portion()
    pass_on(2)
    pass_on(3)
    hear(2)
    tell(3)
    arrive(0)
    response_keys(0)
    arrive(1)
    response_keys(1)
    give_back_far(2)
    arrive(2)
    response_values(0)
    give_back_far(3)
    arrive(3)
    response_values(1)
    sum_gains()
    hear(3)
    start_a()
    give_back_far(0)
    give_back_far(1)
    give_back_near(2)
    give_back_near(3)
    part_a[...] = collect_a()
    start_b()
    give_back_near(0)
    give_back_near(1)
    finish_a()
    for c in range(chunks):
        hop(c).wait_send()
        relay(c).wait_send()
        across(c, 0, 0).wait_send()
        across(c, 1, 0).wait_send()
        back_across(c).wait_send()
        back_far(c).wait_send()
    for c in range(heads, chunks):
        back_near(c).wait_send()
    for h in range(heads):
        finish_values(h)
    for h in range(heads):
        finish_keys(h)
    gains_out[...] = collect_b()

    finish_b()
    back_near(0).wait_send()
    back_near(1).wait_send()


def hand_out(q, k, v, gains, q_out, k_out, v_out, qg_out, kg_out, sems):
    copies = [
        pltpu.make_async_copy(src, dst, sems.at[i])
        for i, (src, dst) in enumerate(
            [
                *[(q.at[r], q_out.at[r]) for r in (pl.ds(96 * i, 96) for i in range(4))],
                (k, k_out),
                (v, v_out),
                (gains.at[0:1], qg_out),
                (gains.at[1:2], kg_out),
            ]
        )
    ]
    for copy in copies:
        copy.start()
    for copy in copies:
        copy.wait()


def on_device(
    n_dp, n_tensor, queries, keys, values, output_gradient, q_gain, k_gain, prompt_len, resp_len, resp_owner
):
    heads = keys.shape[1] // HEAD
    groups = queries.shape[1] // keys.shape[1]
    rows = queries.shape[0]
    chunks = 2 * heads
    n_a = n_dp // 16 * n_tensor
    vmem = pl.BlockSpec(memory_space=pltpu.VMEM)
    smem = pl.BlockSpec(memory_space=pltpu.SMEM)
    hbm = pl.BlockSpec(memory_space=pltpu.HBM)
    asked = groups * RESP
    scratch = [
        pltpu.VMEM(queries.shape, BF16),
        pltpu.VMEM(queries.shape, BF16),
        pltpu.SMEM((1,), jnp.int32),
        pltpu.VMEM(keys.shape, BF16),
        pltpu.VMEM(keys.shape, BF16),
        pltpu.VMEM((5, PROMPT + 16, HEAD), BF16),
        pltpu.VMEM((5, PROMPT, HEAD), BF16),
        pltpu.VMEM((5, PROMPT, HEAD), BF16),
        pltpu.VMEM((5, PROMPT, HEAD), BF16),
        pltpu.VMEM((HEAD, HEAD), BF16),
        pltpu.VMEM((HEAD, HEAD), F32),
        pltpu.VMEM((PROMPT // 2, PROMPT), F32),
        pltpu.VMEM((PROMPT, PROMPT), F32),
        pltpu.VMEM((RESP, HEAD), F32),
        pltpu.VMEM((heads, PROMPT, HEAD), BF16),
        pltpu.VMEM((heads, HEAD, PROMPT), BF16),
        pltpu.VMEM((heads, PROMPT, HEAD), F32),
        pltpu.VMEM((heads, PROMPT, HEAD), F32),
        pltpu.VMEM((HEAD, HEAD), F32),
        pltpu.VMEM((8, HEAD), F32),
        pltpu.VMEM((heads, 2, asked, HEAD), BF16),
        pltpu.VMEM((heads, 2, HEAD, asked), F32),
        pltpu.VMEM((heads, 2, HEAD, asked), BF16),
        pltpu.VMEM((heads, 2, 8, asked), F32),
        pltpu.VMEM((heads, 2, KEYS, HEAD), BF16),
        pltpu.VMEM((heads, 2, HEAD, KEYS), BF16),
        pltpu.VMEM((heads, 2, KEYS, HEAD), F32),
        pltpu.VMEM((heads, 2, KEYS, asked), F32),
        pltpu.VMEM((chunks, 4, PROMPT, HEAD), BF16),
        pltpu.VMEM((chunks, 2, PROMPT, HEAD), BF16),
        pltpu.VMEM((chunks, PROMPT, HEAD), BF16),
        pltpu.VMEM((chunks, PROMPT, HEAD), BF16),
        pltpu.VMEM((chunks, PROMPT, HEAD), BF16),
        pltpu.VMEM((chunks, PROMPT, HEAD), BF16),
        pltpu.VMEM((8, HEAD), F32),
        pltpu.VMEM((8, HEAD), F32),
        pltpu.VMEM((n_a, 8, HEAD), F32),
        pltpu.VMEM((16, 8, HEAD), F32),
        pltpu.SemaphoreType.REGULAR((4, 6)),
        pltpu.SemaphoreType.DMA((chunks + 3 + 2 * heads,)),
        pltpu.SemaphoreType.DMA((4, chunks)),
        pltpu.SemaphoreType.DMA((4, chunks)),
        pltpu.SemaphoreType.DMA((3, chunks)),
        pltpu.SemaphoreType.DMA((3, chunks)),
        pltpu.SemaphoreType.DMA((n_a,)),
        pltpu.SemaphoreType.DMA((n_a,)),
        pltpu.SemaphoreType.DMA((16,)),
        pltpu.SemaphoreType.DMA((16,)),
    ]
    results = pl.pallas_call(
        functools.partial(kernel, heads, groups, n_dp, n_tensor),
        out_shape=(
            pltpu.VMEM(queries.shape, BF16),
            pltpu.VMEM(keys.shape, BF16),
            pltpu.VMEM(keys.shape, BF16),
            pltpu.VMEM((8, HEAD), F32),
        ),
        in_specs=[hbm, smem, smem, vmem, vmem, hbm, hbm, hbm, hbm],
        out_specs=(vmem, vmem, vmem, vmem),
        scratch_shapes=scratch,
        compiler_params=pltpu.CompilerParams(
            collective_id=0, has_side_effects=True, vmem_limit_bytes=56 * 2**20
        ),
        name="attention",
    )(
        prompt_len,
        resp_len,
        resp_owner,
        q_gain.reshape(1, HEAD),
        k_gain.reshape(1, HEAD),
        *[
            pltpu.with_memory_space_constraint(a, pltpu.HBM)
            for a in (queries, keys, values, output_gradient)
        ],
    )
    q_grad, k_grad, v_grad, q_gain_grad, k_gain_grad = pl.pallas_call(
        hand_out,
        out_shape=(
            jax.ShapeDtypeStruct(queries.shape, BF16),
            jax.ShapeDtypeStruct(keys.shape, BF16),
            jax.ShapeDtypeStruct(keys.shape, BF16),
            jax.ShapeDtypeStruct((1, HEAD), F32),
            jax.ShapeDtypeStruct((1, HEAD), F32),
        ),
        in_specs=[vmem] * 4,
        out_specs=(hbm,) * 5,
        scratch_shapes=[pltpu.SemaphoreType.DMA((8,))],
        compiler_params=pltpu.CompilerParams(vmem_limit_bytes=16 * 2**20),
        name="hand_out",
    )(*[pltpu.with_memory_space_constraint(x, pltpu.VMEM) for x in results])
    return q_grad, k_grad, v_grad, q_gain_grad.reshape(HEAD), k_gain_grad.reshape(HEAD)


def solution(mesh):
    rows, whole = P("dp", "tensor"), P()
    return jax.shard_map(
        functools.partial(on_device, mesh.shape["dp"], mesh.shape["tensor"]),
        mesh=mesh,
        in_specs=(rows, rows, rows, rows, whole, whole, P("dp"), P("dp"), P("dp")),
        out_specs=(rows, rows, rows, whole, whole),
        check_vma=False,
    )
```
